512 devices in a mesh: lon: 32 (over y_lo, z, core), lat: 16 (over y_hi, x).
Axes of the slice: x: 4, y: 8 (y_hi: 4, y_lo: 2; y = y_hi * 2 + y_lo), z: 8, core: 2. Of those that a mesh axis runs over, the one named last changes fastest.
Arguments:
- queries: bfloat16 [256, 256, 1024], P('lat', 'lon'), may hold values from -6 to 6
- keys: bfloat16 [256, 256, 1024], P('lat', 'lon'), may hold values from -6 to 6
- values: bfloat16 [256, 256, 1024], P('lat', 'lon'), may hold values from -6 to 6
- cotangent: bfloat16 [256, 256, 1024], P('lat', 'lon'), may hold values from -6 to 6
Outputs:
- attended: bfloat16 [256, 256, 1024], P('lat', 'lon')
- grad_queries: bfloat16 [256, 256, 1024], P('lat', 'lon')
- grad_keys: bfloat16 [256, 256, 1024], P('lat', 'lon')
- grad_values: bfloat16 [256, 256, 1024], P('lat', 'lon')
The draws below stay inside these ranges and needn't reach their ends.
All inputs are finite; a program needn't handle non-finite values.
Results may differ from the reference program's by a relative error of at most 0.0076.
Values may be sent and summed in bfloat16 or wider, within the bound.
A program may use at most 64 MiB of HBM per device.

```python
import jax
import jax.numpy as jnp
from jax import lax

D = 1024
HEADS = 16
RADIUS = 6
ROWS_DEV = 16
COLS_DEV = 8
ROWS = 256
COLS = 256
N_LON = 32
N_LAT = 16


def draw_queries(key, part):
    key = jax.random.fold_in(key, 1)
    base = jnp.clip(jax.random.normal(key, (ROWS, COLS, D), jnp.float32), -6.0, 6.0)
    return base.astype(jnp.bfloat16)


def draw_keys(key, part):
    key = jax.random.fold_in(key, 2)
    base = jnp.clip(jax.random.normal(key, (ROWS, COLS, D), jnp.float32), -6.0, 6.0)
    return base.astype(jnp.bfloat16)


def block_scale(stream_key, extent, split, low, top_value):
    gain = 1.0
    for axis_at, shards_of in split:
        steps = jax.random.uniform(jax.random.fold_in(jax.random.fold_in(stream_key, 6), axis_at), (shards_of,), jnp.float32, low / len(split), top_value / len(split))
        gain = gain * jnp.repeat(jnp.exp(steps), extent[axis_at] // shards_of).reshape((-1,) + (1,) * (len(extent) - 1 - axis_at))
    return gain


def noise(rng, dims, spread, reach, cuts=(), held_as=jnp.bfloat16):
    gain = block_scale(rng, dims, cuts, -0.22, 0.18) if cuts else 1.0
    entries = jax.random.normal(rng, dims, jnp.float32) * spread * gain
    return jnp.minimum(jnp.maximum(entries, -reach), reach).astype(held_as)


def setup_inputs(seed: int = 0) -> dict:
    splits = jax.random.split(jax.random.key(seed), 5)
    return {
        "queries": draw_queries(jax.random.fold_in(splits[4], 71), 0),
        "keys": draw_keys(jax.random.fold_in(splits[4], 71), 0),
        "values": noise(splits[2], (ROWS, COLS, D), 1.0, 6.0, ((0, 16), (1, 32))),
        "cotangent": noise(splits[3], (ROWS, COLS, D), 1.0, 6.0, ((0, 16), (1, 32))),
    }


def window_mask(query_row, query_col, key_row, key_col, total_rows):
    start = jnp.clip(query_row - RADIUS, 0, total_rows - 2 * RADIUS - 1)
    inside = (key_row[None, :] >= start[:, None]) & (key_row[None, :] <= start[:, None] + 2 * RADIUS)
    near = jnp.abs(key_col[None, :] - query_col[:, None]) <= RADIUS
    valid = (query_row >= 0) & (query_row < total_rows)
    return inside & near & valid[:, None]


def tile_terms(query_blk, key_blk, value_blk, cot_blk, mask, scale):
    scores = jnp.einsum('nhd,ehd->hne', query_blk, key_blk) * scale
    scores = jnp.where(mask[None], scores, -jnp.inf)
    highest = jnp.max(scores, axis=2, keepdims=True)
    log_norm = highest + jnp.log(jnp.sum(jnp.exp(scores - highest), axis=2, keepdims=True))
    weights = jnp.exp(scores - log_norm)
    rounded = lax.optimization_barrier(weights.astype(jnp.bfloat16)).astype(jnp.float32)
    attended = jnp.einsum('hne,ehd->nhd', rounded, value_blk)
    weight_grads = jnp.einsum('nhd,ehd->hne', cot_blk, value_blk)
    delta = jnp.sum(weights * weight_grads, axis=2, keepdims=True)
    score_grads = lax.optimization_barrier((weights * (weight_grads - delta)).astype(jnp.bfloat16)).astype(jnp.float32)
    grad_query = jnp.einsum('hne,ehd->nhd', score_grads, key_blk) * scale
    grad_key = jnp.einsum('hne,nhd->ehd', score_grads, query_blk) * scale
    grad_value = jnp.einsum('hne,nhd->ehd', rounded, cot_blk)
    return attended, grad_query, grad_key, grad_value


def reference(queries, keys, values, cotangent):
    head_dim = D // HEADS
    scale = head_dim ** -0.5
    ext_rows = ROWS_DEV + 2 * RADIUS
    ext_cols = COLS_DEV + 2 * RADIUS
    local_rows = jnp.repeat(jnp.arange(ROWS_DEV, dtype=jnp.int32), COLS_DEV)
    local_cols = jnp.tile(jnp.arange(COLS_DEV, dtype=jnp.int32), ROWS_DEV) + RADIUS
    rim_rows = jnp.repeat(jnp.arange(ext_rows, dtype=jnp.int32), ext_cols) - RADIUS
    rim_cols = jnp.tile(jnp.arange(ext_cols, dtype=jnp.int32), ext_rows)
    zero_index = jnp.zeros((), jnp.int32)

    def one_tile(carry, index):
        acc_keys, acc_values = carry
        band = (index // N_LON).astype(jnp.int32)
        slot = (index % N_LON).astype(jnp.int32)
        row_zero = (band * ROWS_DEV).astype(jnp.int32)
        col_zero = (slot * COLS_DEV).astype(jnp.int32)
        take_rows = jnp.clip(row_zero - RADIUS + jnp.arange(ext_rows, dtype=jnp.int32), 0, ROWS - 1).astype(jnp.int32)
        take_cols = jnp.mod(col_zero - RADIUS + jnp.arange(ext_cols, dtype=jnp.int32), COLS).astype(jnp.int32)

        def beside_all(field):
            block = jnp.take(jnp.take(field, take_rows, axis=0), take_cols, axis=1)
            return block.astype(jnp.float32).reshape(ext_rows * ext_cols, HEADS, head_dim)

        def inside(field):
            block = lax.dynamic_slice(field, (row_zero, col_zero, zero_index), (ROWS_DEV, COLS_DEV, D))
            return block.astype(jnp.float32).reshape(ROWS_DEV * COLS_DEV, HEADS, head_dim)

        mask = window_mask(row_zero + local_rows, local_cols, row_zero + rim_rows, rim_cols, ROWS)
        attended, grad_query, grad_key, grad_value = tile_terms(
            inside(queries), beside_all(keys), beside_all(values), inside(cotangent), mask, scale)
        acc_keys = acc_keys.at[take_rows[:, None], take_cols[None, :]].add(grad_key.reshape(ext_rows, ext_cols, D))
        acc_values = acc_values.at[take_rows[:, None], take_cols[None, :]].add(grad_value.reshape(ext_rows, ext_cols, D))
        outputs = (attended.reshape(ROWS_DEV, COLS_DEV, D).astype(jnp.bfloat16),
                   grad_query.reshape(ROWS_DEV, COLS_DEV, D).astype(jnp.bfloat16))
        return (acc_keys, acc_values), outputs

    start_acc = (jnp.zeros((ROWS, COLS, D), jnp.float32), jnp.zeros((ROWS, COLS, D), jnp.float32))
    (acc_keys, acc_values), (tiles_out, tiles_dq) = lax.scan(
        one_tile, start_acc, jnp.arange(N_LAT * N_LON, dtype=jnp.int32))

    def assemble(blocks):
        return blocks.reshape(N_LAT, N_LON, ROWS_DEV, COLS_DEV, D).transpose(0, 2, 1, 3, 4).reshape(ROWS, COLS, D)

    return (assemble(tiles_out), assemble(tiles_dq),
            acc_keys.astype(jnp.bfloat16), acc_values.astype(jnp.bfloat16))
```

```python
import functools

import jax
import jax.numpy as jnp
from jax import lax
from jax.experimental import pallas as pl
from jax.experimental.pallas import tpu as pltpu
from jax.sharding import PartitionSpec as P

RADIUS = 6
HEAD = 64
ROWS = 16
COLS = 8
OWN = ROWS * COLS
NN, SS, WW, EE, WC, EC, EXT = 128, 176, 224, 320, 416, 496, 576
LOG2E = 1.4426950408889634
NEG = -1e30
F32, BF16, I32 = jnp.float32, jnp.bfloat16, jnp.int32
MESH = pl.DeviceIdType.MESH
NEIGHBOURS = [(a, b) for a in (-1, 0, 1) for b in (-1, 0, 1) if (a, b) != (0, 0)]


def iota(shape, dim):
    return lax.broadcasted_iota(I32, shape, dim)


def div6(x):
    return (x * 171) >> 10


def ext_coords(e):
    j = e - WW
    r6 = div6(jnp.maximum(j, 0))
    row = r6
    col = j - 6 * r6 - 6
    j = e - EE
    r6 = div6(jnp.maximum(j, 0))
    row = jnp.where(e >= EE, r6, row)
    col = jnp.where(e >= EE, j - 6 * r6 + COLS, col)
    row = jnp.where(e < WW, ROWS + ((e - SS) >> 3), row)
    row = jnp.where(e < SS, ((e - NN) >> 3) - RADIUS, row)
    row = jnp.where(e < NN, e >> 3, row)
    col = jnp.where(e < WW, e & 7, col)
    j = jnp.where(e >= EC, e - EC, e - WC)
    low = j >= 40
    j = jnp.maximum(jnp.where(low, j - 40, j), 0)
    r6 = div6(j)
    ok = (e < WC) | (j < 36)
    row = jnp.where(e >= WC, jnp.where(low, ROWS + r6, r6 - RADIUS), row)
    col = jnp.where(e >= WC, j - 6 * r6 + jnp.where(e >= EC, COLS, -RADIUS), col)
    return row, col, ok


def pack_matrix(first_col):
    i = iota((96, OWN), 0)
    r = div6(i)
    src = r * 8 + (i - 6 * r) + first_col
    return jnp.where(iota((96, OWN), 1) == src, 1.0, 0.0).astype(BF16)


def corner_matrix(first_col):
    i = iota((80, 96), 0)
    low = i >= 40
    j = jnp.where(low, i - 40, i)
    r = div6(j)
    src = r * 8 + (j - 6 * r) + first_col + jnp.where(low, 48, 0)
    src = jnp.where(j < 36, src, -1)
    return jnp.where(iota((80, 96), 1) == src, 1.0, 0.0).astype(BF16)


def dot_t(a, b):
    return lax.dot_general(a, b, (((1,), (1,)), ((), ())), preferred_element_type=F32)


def dot(a, b):
    return jnp.dot(a, b, preferred_element_type=F32)


def kernel(n_lat, n_lon, pairs, q_ref, k_ref, v_ref, c_ref, o_ref, dq_ref, dk_ref, dv_ref,
           ext, snd_side, snd_corner, bias1, bias2, perm, stat_acc, stat_own, stat_in, stat_ext,
           send_sem, recv_sem, stat_send, stat_recv):
    lat, lon = lax.axis_index("lat"), lax.axis_index("lon")
    heads = 2 * pairs
    total_rows = n_lat * ROWS
    first = lat * ROWS
    scale = HEAD ** -0.5

    def device(a, b):
        return {"lat": lax.rem(lat + a + n_lat, n_lat), "lon": lax.rem(lon + b + n_lon, n_lon)}

    barrier = pltpu.get_barrier_semaphore()
    for a, b in NEIGHBOURS:
        pl.semaphore_signal(barrier, inc=1, device_id=device(a, b), device_id_type=MESH)

    def remote(src, dst, sem, to):
        return pltpu.make_async_remote_copy(
            src_ref=src, dst_ref=dst, send_sem=send_sem.at[sem], recv_sem=recv_sem.at[sem],
            device_id=to, device_id_type=MESH)

    def strips(s):
        at = pl.ds(2 * s, 2)
        return [
            remote(ext.at[at, :, pl.ds(0, 48)], ext.at[at, :, pl.ds(SS, 48)], 6 * s, device(-1, 0)),
            remote(ext.at[at, :, pl.ds(80, 48)], ext.at[at, :, pl.ds(NN, 48)], 6 * s + 1, device(1, 0)),
        ]

    def sides(s):
        at = pl.ds(2 * s, 2)
        return [
            remote(snd_side.at[0, at], ext.at[at, :, pl.ds(WW, 96)], 6 * s + 2, device(0, 1)),
            remote(snd_side.at[1, at], ext.at[at, :, pl.ds(EE, 96)], 6 * s + 3, device(0, -1)),
        ]

    def corners(s):
        at = pl.ds(2 * s, 2)
        return [
            remote(snd_corner.at[0, at], ext.at[at, :, pl.ds(WC, 80)], 6 * s + 4, device(0, 1)),
            remote(snd_corner.at[1, at], ext.at[at, :, pl.ds(EC, 80)], 6 * s + 5, device(0, -1)),
        ]

    def start(copies):
        for copy in copies:
            copy.start()

    def pack(s):
        east, west = pack_matrix(2), pack_matrix(0)
        for a, ref in ((2 * s, (k_ref, q_ref)[s]), (2 * s + 1, (v_ref, c_ref)[s])):
            for p in range(pairs):
                block = ref[:, 128 * p:128 * (p + 1)]
                ext[a, p, 0:OWN, :] = block
                snd_side[0, a, p] = dot(east, block).astype(BF16)
                snd_side[1, a, p] = dot(west, block).astype(BF16)

    def pack_corners(s):
        east, west = corner_matrix(2), corner_matrix(0)
        for a in (2 * s, 2 * s + 1):
            for p in range(pairs):
                block = ext[a, p, NN:WW, :]
                snd_corner[0, a, p] = dot(east, block).astype(BF16)
                snd_corner[1, a, p] = dot(west, block).astype(BF16)

    pack(0)
    pl.semaphore_wait(barrier, len(NEIGHBOURS))
    start(strips(0))
    start(sides(0))
    pack(1)
    start(strips(1))
    start(sides(1))

    row, col, ok = ext_coords(iota((OWN, EXT), 1))
    own = iota((OWN, EXT), 0)
    near = (jnp.abs(col - (own & 7)) <= RADIUS) & ok
    own_row = first + (own >> 3)
    ext_row = first + row
    begin = jnp.clip(own_row - RADIUS, 0, total_rows - 2 * RADIUS - 1)
    inside = near & (ext_row >= begin) & (ext_row <= begin + 2 * RADIUS)
    bias1[...] = jnp.where(inside, 0.0, NEG)
    begin = jnp.clip(ext_row - RADIUS, 0, total_rows - 2 * RADIUS - 1)
    inside = near & (own_row >= begin) & (own_row <= begin + 2 * RADIUS)
    inside = inside & (ext_row >= 0) & (ext_row < total_rows)
    bias2[...] = jnp.where(inside, 0.0, NEG)

    row, col, ok = ext_coords(iota((8, EXT), 1))
    above, below = row < 0, row >= ROWS
    left, right = col < 0, col >= COLS
    part = 4 + jnp.where(above, -3, 0) + jnp.where(below, 3, 0) + jnp.where(left, -1, 0) + jnp.where(right, 1, 0)
    src = part * OWN + (row & (ROWS - 1)) * 8 + (col & (COLS - 1))
    src = jnp.where(ok, src, -1)[0:1]
    for b in range(9):
        at = iota((OWN, EXT), 0) + b * OWN
        perm[b * OWN:(b + 1) * OWN, :] = jnp.where(at == src, 1.0, 0.0).astype(BF16)

    for copy in strips(0):
        copy.wait_recv()
    pack_corners(0)
    start(corners(0))
    for copy in strips(1):
        copy.wait_recv()
    pack_corners(1)
    start(corners(1))

    lane = iota((1, 128), 1)
    lo = jnp.where(lane < HEAD, 1.0, 0.0).astype(BF16)
    hi = jnp.where(lane < HEAD, 0.0, 1.0).astype(BF16)
    lower = iota((OWN, 128), 1) < HEAD

    def by_head(x):
        return jnp.concatenate([x * lo, x * hi], axis=0)

    def merged(x):
        return jnp.where(lower, x[:OWN], x[OWN:])

    def lanes(p):
        return pl.ds(pl.multiple_of(p * 128, 128), 128)

    for copy in sides(0) + corners(0):
        copy.wait_recv()

    stat_acc[...] = jnp.zeros_like(stat_acc)

    def forward(p, carry):
        kx, vx = ext[0, p], ext[1, p]
        qs = by_head(ext[2, p, 0:OWN, :])
        cs = by_head(ext[3, p, 0:OWN, :])
        s = dot_t(qs, kx)
        dw = dot_t(cs, vx)
        rounded, grads = [], []
        lane_at = iota((OWN, 128), 1)
        acc = stat_acc[...]
        for h in range(2):
            part = slice(h * OWN, (h + 1) * OWN)
            t = s[part] * (scale * LOG2E) + bias1[...]
            m = jnp.max(t, axis=1, keepdims=True)
            e = jnp.exp2(t - m)
            total = jnp.sum(e, axis=1, keepdims=True)
            w = e * (1.0 / total)
            rounded.append(w.astype(BF16))
            g = dw[part]
            delta = jnp.sum(w * g, axis=1, keepdims=True)
            grads.append((w * (g - delta)).astype(BF16))
            acc = jnp.where(lane_at == 2 * p + h, m + jnp.log2(total), acc)
            acc = jnp.where(lane_at == heads + 2 * p + h, delta, acc)
        stat_acc[...] = acc
        o = dot(jnp.concatenate(rounded, axis=0), vx)
        dq = dot(jnp.concatenate(grads, axis=0), kx)
        o_ref[:, lanes(p)] = merged(o).astype(BF16)
        dq_ref[:, lanes(p)] = (merged(dq) * scale).astype(BF16)
        return carry

    lax.fori_loop(0, pairs, forward, 0)

    stat_own[...] = stat_acc[...].T[0:2 * heads]

    def stat_copy(i, to):
        return pltpu.make_async_remote_copy(
            src_ref=stat_own, dst_ref=stat_in.at[i], send_sem=stat_send.at[i], recv_sem=stat_recv.at[i],
            device_id=to, device_id_type=MESH)

    stats = [stat_copy(i, device(-a, -b)) for i, (a, b) in enumerate(NEIGHBOURS)]
    start(stats)

    for copy in sides(1) + corners(1):
        copy.wait_recv()
    for copy in stats:
        copy.wait_recv()

    blocks = [stat_in[i] for i in range(8)]
    blocks = blocks[:4] + [stat_own[...]] + blocks[4:]
    x = jnp.concatenate(blocks, axis=1)
    x1 = x.astype(BF16)
    rest = x - x1.astype(F32)
    x2 = rest.astype(BF16)
    x3 = (rest - x2.astype(F32)).astype(BF16)
    y = dot(jnp.concatenate([x1, x2, x3], axis=0), perm[...])
    y = (y[0:2 * heads] + y[2 * heads:4 * heads]) + y[4 * heads:6 * heads]
    for i in range(2 * heads):
        stat_ext[i] = y[i:i + 1]

    def backward(p, carry):
        qx, cx = ext[2, p], ext[3, p]
        ks = by_head(ext[0, p, 0:OWN, :])
        vs = by_head(ext[1, p, 0:OWN, :])
        s = dot_t(ks, qx)
        dw = dot_t(vs, cx)
        rounded, grads = [], []
        for h in range(2):
            part = slice(h * OWN, (h + 1) * OWN)
            norm = stat_ext[2 * p + h]
            delta = stat_ext[heads + 2 * p + h]
            w = jnp.exp2(s[part] * (scale * LOG2E) + bias2[...] - norm)
            rounded.append(w.astype(BF16))
            grads.append((w * (dw[part] - delta)).astype(BF16))
        dv = dot(jnp.concatenate(rounded, axis=0), cx)
        dk = dot(jnp.concatenate(grads, axis=0), qx)
        dv_ref[:, lanes(p)] = merged(dv).astype(BF16)
        dk_ref[:, lanes(p)] = (merged(dk) * scale).astype(BF16)
        return carry

    lax.fori_loop(0, pairs, backward, 0)

    for s in range(2):
        for copy in strips(s) + sides(s) + corners(s):
            copy.wait_send()
    for copy in stats:
        copy.wait_send()


def solution(mesh):
    n_lat, n_lon = mesh.shape["lat"], mesh.shape["lon"]

    def shards(queries, keys, values, cotangent):
        width = queries.shape[2]
        pairs = width // 128
        heads = 2 * pairs
        flat = [x.reshape(OWN, width) for x in (queries, keys, values, cotangent)]
        outs = pl.pallas_call(
            functools.partial(kernel, n_lat, n_lon, pairs),
            out_shape=[jax.ShapeDtypeStruct((OWN, width), BF16)] * 4,
            in_specs=[pl.BlockSpec(memory_space=pltpu.VMEM)] * 4,
            out_specs=[pl.BlockSpec(memory_space=pltpu.VMEM)] * 4,
            scratch_shapes=[
                pltpu.VMEM((4, pairs, EXT, 128), BF16),
                pltpu.VMEM((2, 4, pairs, 96, 128), BF16),
                pltpu.VMEM((2, 4, pairs, 80, 128), BF16),
                pltpu.VMEM((OWN, EXT), F32),
                pltpu.VMEM((OWN, EXT), F32),
                pltpu.VMEM((9 * OWN, EXT), BF16),
                pltpu.VMEM((OWN, 128), F32),
                pltpu.VMEM((2 * heads, OWN), F32),
                pltpu.VMEM((8, 2 * heads, OWN), F32),
                pltpu.VMEM((2 * heads, 1, EXT), F32),
                pltpu.SemaphoreType.DMA((12,)),
                pltpu.SemaphoreType.DMA((12,)),
                pltpu.SemaphoreType.DMA((8,)),
                pltpu.SemaphoreType.DMA((8,)),
            ],
            compiler_params=pltpu.CompilerParams(
                collective_id=0, has_side_effects=True, vmem_limit_bytes=48 * 1024 * 1024),
        )(*flat)
        return tuple(x.reshape(ROWS, COLS, width) for x in outs)

    spec = P("lat", "lon", None)
    return jax.shard_map(shards, mesh=mesh, in_specs=(spec,) * 4, out_specs=(spec,) * 4, check_vma=False)
```

```python
import functools

import jax
import jax.numpy as jnp
from jax import lax
from jax.experimental import pallas as pl
from jax.experimental.pallas import tpu as pltpu
from jax.sharding import PartitionSpec as P

RADIUS = 6
HEAD = 64
ROWS = 16
COLS = 8
OWN = ROWS * COLS
HALF = OWN // 2
NN, CN, MID, WW, EE, SS, CS, EXT = 0, 48, 128, 256, 352, 448, 496, 576
SPAN = 448
SEGMENTS = [
    (0, 8, -6, 0, 48), (48, 6, -6, -6, 36), (88, 6, -6, 8, 36), (128, 8, 0, 0, 128), (256, 6, 0, -6, 96),
    (352, 6, 0, 8, 96), (448, 8, 16, 0, 48), (496, 6, 16, 8, 36), (536, 6, 16, -6, 36),
]
XS = 4
LOG2E = 1.4426950408889634
NEG = -1e30
F32, BF16, I32 = jnp.float32, jnp.bfloat16, jnp.int32
MESH = pl.DeviceIdType.MESH
NEIGHBOURS = [(a, b) for a in (-1, 0, 1) for b in (-1, 0, 1) if (a, b) != (0, 0)]
GREETED = NEIGHBOURS + [(a, 0) for a in (-4, -3, -2, 2, 3, 4)]


def iota(shape, dim):
    return lax.broadcasted_iota(I32, shape, dim)


def div6(x):
    return (x * 171) >> 10


def ext_coords(e):
    row = col = ok = None
    for first, wide, row0, col0, count in SEGMENTS:
        j = jnp.maximum(e - first, 0)
        r = (j >> 3) if wide == 8 else div6(j)
        c = j - wide * r + col0
        r = r + row0
        good = jnp.where(j < count, 1, 0)
        if row is None:
            row, col, ok = r, c, good
        else:
            row = jnp.where(e >= first, r, row)
            col = jnp.where(e >= first, c, col)
            ok = jnp.where(e >= first, good, ok)
    return row, col, ok > 0


def pack_matrix(first_col):
    i = iota((96, OWN), 0)
    r = div6(i)
    src = r * 8 + (i - 6 * r) + first_col
    return jnp.where(iota((96, OWN), 1) == src, 1.0, 0.0).astype(BF16)


def corner_matrix(first_col, swapped):
    i = iota((80, 96), 0)
    second = i >= 40
    j = jnp.where(second, i - 40, i)
    r = div6(j)
    from_below = jnp.where(second, 0, 48) if swapped else jnp.where(second, 48, 0)
    src = r * 8 + (j - 6 * r) + first_col + from_below
    src = jnp.where(j < 36, src, -1)
    return jnp.where(iota((80, 96), 1) == src, 1.0, 0.0).astype(BF16)


def dot_t(a, b):
    return lax.dot_general(a, b, (((1,), (1,)), ((), ())), preferred_element_type=F32)


def dot(a, b):
    return jnp.dot(a, b, preferred_element_type=F32)


def kernel(n_lat, n_lon, pairs, q_hbm, k_hbm, v_hbm, c_hbm, o_ref, dq_ref, dk_ref, dv_ref,
           inputs, ext, snd_side, snd_corner, rcv_corner, relay, bias1, bias2, perm, stat_acc, stat_own, stat_in,
           stat_ext, in_sem, side_s, side_r, corner_s, corner_r, strip_s, strip_r, relay_r, pass_s,
           stat_s, stat_r):
    lat, lon = lax.axis_index("lat"), lax.axis_index("lon")
    x = lax.rem(lat, XS)
    heads = 2 * pairs
    half = pairs // 2
    total_rows = n_lat * ROWS
    first = lat * ROWS
    scale = HEAD ** -0.5

    def device(a, b):
        return {"lat": lax.rem(lat + a + n_lat, n_lat), "lon": lax.rem(lon + b + n_lon, n_lon)}

    barrier = pltpu.get_barrier_semaphore()
    for a, b in GREETED:
        pl.semaphore_signal(barrier, inc=1, device_id=device(a, b), device_id_type=MESH)

    loads = [pltpu.make_async_copy(ref, inputs.at[i], in_sem.at[i])
             for i, ref in enumerate((k_hbm, v_hbm, q_hbm, c_hbm))]
    for load in loads:
        load.start()

    def remote(src, dst, send, recv, to):
        return pltpu.make_async_remote_copy(
            src_ref=src, dst_ref=dst, send_sem=send, recv_sem=recv, device_id=to, device_id_type=MESH)

    def arrays(c):
        return pl.ds(2 * (c // 2), 2)

    def heads_of(c):
        return pl.ds(half * (c % 2), half)

    def strip(c, d):
        src = ext.at[arrays(c), heads_of(c), pl.ds(MID + 80 if d == 0 else MID, 48)]
        dst = ext.at[arrays(c), heads_of(c), pl.ds(NN if d == 0 else SS, 48)]
        return remote(src, dst, strip_s.at[c, d, 0], strip_r.at[c, d, 0], device(1 if d == 0 else -1, 0))

    def part(c, d, j):
        at = (arrays(c), half * (c % 2) + j)
        src = ext.at[*at, pl.ds(MID + 80 if d == 0 else MID, 48)]
        to = device(1 + j, 0) if d == 0 else device(-4 + j, 0)
        if j == (0 if d == 0 else XS - 1):
            dst = ext.at[*at, pl.ds(NN if d == 0 else SS, 48)]
            return remote(src, dst, strip_s.at[c, d, j], strip_r.at[c, d, j], to)
        return remote(src, relay.at[c, d], strip_s.at[c, d, j], relay_r.at[c, d], to)

    def passed(c, d):
        dst = ext.at[arrays(c), half * (c % 2) + x, pl.ds(NN if d == 0 else SS, 48)]
        return remote(relay.at[c, d], dst, pass_s.at[c, d], strip_r.at[c, d, x],
                      device(-x, 0) if d == 0 else device(XS - 1 - x, 0))

    def landed(c, d, j):
        dst = ext.at[arrays(c), half * (c % 2) + j, pl.ds(NN if d == 0 else SS, 48)]
        return remote(relay.at[c, d], dst, pass_s.at[c, d], strip_r.at[c, d, j], device(1, 0))

    last = (XS - 1, 0)

    def start_strips(c):
        for d in range(2):
            @pl.when(x != last[d])
            def _():
                strip(c, d).start()

            @pl.when(x == last[d])
            def _():
                for j in range(XS):
                    part(c, d, j).start()

    def pass_on(c):
        for d in range(2):
            @pl.when(x != last[1 - d])
            def _():
                part(c, d, 1).wait_recv()
                passed(c, d).start()

    def wait_strips(c):
        for d in range(2):
            @pl.when(x != last[1 - d])
            def _():
                strip(c, d).wait_recv()

            @pl.when(x == last[1 - d])
            def _():
                for j in range(XS):
                    landed(c, d, j).wait_recv()

    def sent_strips(c):
        for d in range(2):
            @pl.when(x != last[d])
            def _():
                strip(c, d).wait_send()

            @pl.when(x == last[d])
            def _():
                for j in range(XS):
                    part(c, d, j).wait_send()

            @pl.when(x != last[1 - d])
            def _():
                passed(c, d).wait_send()

    def sides(c):
        return [remote(snd_side.at[i, arrays(c), heads_of(c)], ext.at[arrays(c), heads_of(c), pl.ds(to, 96)],
                       side_s.at[c, i], side_r.at[c, i], device(0, b))
                for i, (to, b) in enumerate(((WW, 1), (EE, -1)))]

    def corners(c):
        return [remote(snd_corner.at[i, arrays(c), heads_of(c)], rcv_corner.at[i, arrays(c), heads_of(c)],
                       corner_s.at[c, i], corner_r.at[c, i], device(0, b))
                for i, b in enumerate((1, -1))]

    def start(copies):
        for copy in copies:
            copy.start()

    def pack(s):
        east, west = pack_matrix(2), pack_matrix(0)
        for a in (2 * s, 2 * s + 1):
            for p in range(pairs):
                block = inputs[a, :, 128 * p:128 * (p + 1)]
                ext[a, p, MID:MID + OWN, :] = block
                snd_side[0, a, p] = dot(east, block).astype(BF16)
                snd_side[1, a, p] = dot(west, block).astype(BF16)

    def pack_corners(c):
        east, west = corner_matrix(2, False), corner_matrix(0, True)
        for a in (2 * (c // 2), 2 * (c // 2) + 1):
            for p in range(half * (c % 2), half * (c % 2) + half):
                block = jnp.concatenate([ext[a, p, NN:NN + 48, :], ext[a, p, SS:SS + 48, :]], axis=0)
                snd_corner[0, a, p] = dot(east, block).astype(BF16)
                snd_corner[1, a, p] = dot(west, block).astype(BF16)

    def place_corners(c):
        for copy in corners(c):
            copy.wait_recv()
        early = iota((80, 128), 0) < 40
        one = jnp.where(early, 1.0, 0.0).astype(BF16)
        two = jnp.where(early, 0.0, 1.0).astype(BF16)
        for a in (2 * (c // 2), 2 * (c // 2) + 1):
            for p in range(half * (c % 2), half * (c % 2) + half):
                w, e = rcv_corner[0, a, p], rcv_corner[1, a, p]
                ext[a, p, CN:CN + 80, :] = w * one + e * two
                ext[a, p, CS:CS + 80, :] = e * one + w * two

    loads[0].wait()
    loads[1].wait()
    pack(0)
    pl.semaphore_wait(barrier, len(GREETED))
    start_strips(0)
    start(sides(0))
    start_strips(1)
    start(sides(1))
    loads[2].wait()
    loads[3].wait()
    pack(1)
    start_strips(2)
    start_strips(3)
    pass_on(0)

    row, col, ok = ext_coords(iota((8, EXT), 1))
    row, col, ok = row[0:1], col[0:1], jnp.where(ok, 1, 0)[0:1]
    for i in range(2):
        e = slice(128 * i, 128 * i + SPAN)
        token = iota((HALF, SPAN), 0) + HALF * i
        near = (jnp.abs(col[:, e] - (token & 7)) <= RADIUS) & (ok[:, e] > 0)
        own_row = first + (token >> 3)
        ext_row = first + row[:, e]
        begin = jnp.clip(own_row - RADIUS, 0, total_rows - 2 * RADIUS - 1)
        inside = near & (ext_row >= begin) & (ext_row <= begin + 2 * RADIUS)
        bias1[HALF * i:HALF * (i + 1), :] = jnp.where(inside, 0.0, NEG)
        begin = jnp.clip(ext_row - RADIUS, 0, total_rows - 2 * RADIUS - 1)
        inside = near & (own_row >= begin) & (own_row <= begin + 2 * RADIUS)
        inside = inside & (ext_row >= 0) & (ext_row < total_rows)
        bias2[HALF * i:HALF * (i + 1), :] = jnp.where(inside, 0.0, NEG)

    pass_on(1)
    wait_strips(0)
    pack_corners(0)
    start(corners(0))
    wait_strips(1)
    pack_corners(1)
    start(corners(1))
    start(sides(2))
    start(sides(3))

    up, down = jnp.where(row < 0, -3, 0), jnp.where(row >= ROWS, 3, 0)
    left, right = jnp.where(col < 0, -1, 0), jnp.where(col >= COLS, 1, 0)
    src = (4 + up + down + left + right) * OWN + (row & (ROWS - 1)) * 8 + (col & (COLS - 1))
    src = jnp.where(ok > 0, src, -1)
    for b in range(9):
        at = iota((OWN, EXT), 0) + b * OWN
        perm[b * OWN:(b + 1) * OWN, :] = jnp.where(at == src, 1.0, 0.0).astype(BF16)

    lane = iota((1, 128), 1)
    lo = jnp.where(lane < HEAD, 1.0, 0.0).astype(BF16)
    hi = jnp.where(lane < HEAD, 0.0, 1.0).astype(BF16)
    lower = iota((HALF, 128), 1) < HEAD

    def by_head(v):
        return jnp.concatenate([v * lo, v * hi], axis=0)

    def merged(v):
        return jnp.where(lower, v[:HALF], v[HALF:])

    def lanes(p):
        return pl.ds(pl.multiple_of(p * 128, 128), 128)

    stat_acc[...] = jnp.zeros_like(stat_acc)

    def forward(p, carry):
        for i in range(2):
            mine = slice(MID + HALF * i, MID + HALF * (i + 1))
            rows = slice(HALF * i, HALF * (i + 1))
            span = slice(128 * i, 128 * i + SPAN)
            kx, vx = ext[0, p, span, :], ext[1, p, span, :]
            s = dot_t(by_head(ext[2, p, mine, :]), kx)
            dw = dot_t(by_head(ext[3, p, mine, :]), vx)
            bias = bias1[rows, :]
            acc = stat_acc[rows, :]
            lane_at = iota((HALF, 128), 1)
            rounded, grads = [], []
            for h in range(2):
                of = slice(h * HALF, (h + 1) * HALF)
                t = s[of] * (scale * LOG2E) + bias
                m = jnp.max(t, axis=1, keepdims=True)
                e = jnp.exp2(t - m)
                total = jnp.sum(e, axis=1, keepdims=True)
                w = e * (1.0 / total)
                rounded.append(w.astype(BF16))
                g = dw[of]
                delta = jnp.sum(w * g, axis=1, keepdims=True)
                grads.append((w * (g - delta)).astype(BF16))
                acc = jnp.where(lane_at == 2 * p + h, m + jnp.log2(total), acc)
                acc = jnp.where(lane_at == heads + 2 * p + h, delta, acc)
            stat_acc[rows, :] = acc
            o = dot(jnp.concatenate(rounded, axis=0), vx)
            dq = dot(jnp.concatenate(grads, axis=0), kx)
            o_ref[rows, lanes(p)] = merged(o).astype(BF16)
            dq_ref[rows, lanes(p)] = (merged(dq) * scale).astype(BF16)
        return carry

    def backward(p, carry):
        for i in range(2):
            mine = slice(MID + HALF * i, MID + HALF * (i + 1))
            rows = slice(HALF * i, HALF * (i + 1))
            span = slice(128 * i, 128 * i + SPAN)
            qx, cx = ext[2, p, span, :], ext[3, p, span, :]
            s = dot_t(by_head(ext[0, p, mine, :]), qx)
            dw = dot_t(by_head(ext[1, p, mine, :]), cx)
            bias = bias2[rows, :]
            rounded, grads = [], []
            for h in range(2):
                of = slice(h * HALF, (h + 1) * HALF)
                norm = stat_ext[2 * p + h][:, span]
                delta = stat_ext[heads + 2 * p + h][:, span]
                w = jnp.exp2(s[of] * (scale * LOG2E) + bias - norm)
                rounded.append(w.astype(BF16))
                grads.append((w * (dw[of] - delta)).astype(BF16))
            dv = dot(jnp.concatenate(rounded, axis=0), cx)
            dk = dot(jnp.concatenate(grads, axis=0), qx)
            dv_ref[rows, lanes(p)] = merged(dv).astype(BF16)
            dk_ref[rows, lanes(p)] = (merged(dk) * scale).astype(BF16)
        return carry

    def wait_sides(c):
        for copy in sides(c):
            copy.wait_recv()

    wait_sides(0)
    place_corners(0)
    lax.fori_loop(0, half, forward, 0)
    pass_on(2)
    pass_on(3)
    wait_strips(2)
    pack_corners(2)
    start(corners(2))
    wait_sides(1)
    place_corners(1)
    lax.fori_loop(half, pairs, forward, 0)

    stat_own[...] = stat_acc[...].T[0:2 * heads]
    stats = [remote(stat_own, stat_in.at[i], stat_s.at[i], stat_r.at[i], device(-a, -b))
             for i, (a, b) in enumerate(NEIGHBOURS)]
    start(stats)
    wait_strips(3)
    pack_corners(3)
    start(corners(3))

    for copy in stats:
        copy.wait_recv()
    blocks = [stat_in[i] for i in range(8)]
    blocks = blocks[:4] + [stat_own[...]] + blocks[4:]
    whole = jnp.concatenate(blocks, axis=1)
    x1 = whole.astype(BF16)
    rest = whole - x1.astype(F32)
    x2 = rest.astype(BF16)
    x3 = (rest - x2.astype(F32)).astype(BF16)
    y = dot(jnp.concatenate([x1, x2, x3], axis=0), perm[...])
    y = (y[0:2 * heads] + y[2 * heads:4 * heads]) + y[4 * heads:6 * heads]
    for i in range(2 * heads):
        stat_ext[i] = y[i:i + 1]

    wait_sides(2)
    place_corners(2)
    lax.fori_loop(0, half, backward, 0)
    wait_sides(3)
    place_corners(3)
    lax.fori_loop(half, pairs, backward, 0)

    for c in range(4):
        sent_strips(c)
        for copy in sides(c) + corners(c):
            copy.wait_send()
    for copy in stats:
        copy.wait_send()


def solution(mesh):
    n_lat, n_lon = mesh.shape["lat"], mesh.shape["lon"]

    def shards(queries, keys, values, cotangent):
        width = queries.shape[2]
        pairs = width // 128
        heads = 2 * pairs
        flat = [x.reshape(OWN, width) for x in (queries, keys, values, cotangent)]
        dma = pltpu.SemaphoreType.DMA
        outs = pl.pallas_call(
            functools.partial(kernel, n_lat, n_lon, pairs),
            out_shape=[jax.ShapeDtypeStruct((OWN, width), BF16)] * 4,
            in_specs=[pl.BlockSpec(memory_space=pltpu.HBM)] * 4,
            out_specs=[pl.BlockSpec(memory_space=pltpu.VMEM)] * 4,
            scratch_shapes=[
                pltpu.VMEM((4, OWN, width), BF16),
                pltpu.VMEM((4, pairs, EXT, 128), BF16),
                pltpu.VMEM((2, 4, pairs, 96, 128), BF16),
                pltpu.VMEM((2, 4, pairs, 80, 128), BF16),
                pltpu.VMEM((2, 4, pairs, 80, 128), BF16),
                pltpu.VMEM((4, 2, 2, 48, 128), BF16),
                pltpu.VMEM((OWN, SPAN), F32),
                pltpu.VMEM((OWN, SPAN), F32),
                pltpu.VMEM((9 * OWN, EXT), BF16),
                pltpu.VMEM((OWN, 128), F32),
                pltpu.VMEM((2 * heads, OWN), F32),
                pltpu.VMEM((8, 2 * heads, OWN), F32),
                pltpu.VMEM((2 * heads, 1, EXT), F32),
                dma((4,)), dma((4, 2)), dma((4, 2)), dma((4, 2)), dma((4, 2)),
                dma((4, 2, XS)), dma((4, 2, XS)), dma((4, 2)), dma((4, 2)), dma((8,)), dma((8,)),
            ],
            compiler_params=pltpu.CompilerParams(
                collective_id=0, has_side_effects=True, vmem_limit_bytes=48 * 1024 * 1024),
        )(*flat)
        return tuple(x.reshape(ROWS, COLS, width) for x in outs)

    spec = P("lat", "lon", None)
    return jax.shard_map(shards, mesh=mesh, in_specs=(spec,) * 4, out_specs=(spec,) * 4, check_vma=False)
```

```python
import functools

import jax
import jax.numpy as jnp
from jax import lax
from jax.experimental import pallas as pl
from jax.experimental.pallas import tpu as pltpu
from jax.sharding import PartitionSpec as P

RADIUS = 6
HEAD = 64
ROWS = 16
COLS = 8
OWN = ROWS * COLS
NN, SS, WW, EE, WC, EC, EXT = 128, 176, 224, 320, 416, 496, 576
SEGMENTS = [
    (0, 8, 0, 0, 128), (128, 8, -6, 0, 48), (176, 8, 16, 0, 48), (224, 6, 0, -6, 96), (320, 6, 0, 8, 96),
    (416, 6, -6, -6, 36), (456, 6, 16, -6, 36), (496, 6, -6, 8, 36), (536, 6, 16, 8, 36),
]
XS = 4
LOG2E = 1.4426950408889634
NEG = -1e30
F32, BF16, I32 = jnp.float32, jnp.bfloat16, jnp.int32
MESH = pl.DeviceIdType.MESH
GREETED = [(1, 0), (-1, 0), (4, 0), (-4, 0), (0, 1), (0, -1)]


def iota(shape, dim):
    return lax.broadcasted_iota(I32, shape, dim)


def div6(x):
    return (x * 171) >> 10


def ext_coords(e):
    row = col = ok = None
    for first, wide, row0, col0, count in SEGMENTS:
        j = jnp.maximum(e - first, 0)
        r = (j >> 3) if wide == 8 else div6(j)
        c = j - wide * r + col0
        r = r + row0
        good = jnp.where(j < count, 1, 0)
        if row is None:
            row, col, ok = r, c, good
        else:
            row = jnp.where(e >= first, r, row)
            col = jnp.where(e >= first, c, col)
            ok = jnp.where(e >= first, good, ok)
    return row, col, ok > 0


def pack_matrix(first_col):
    i = iota((96, OWN), 0)
    r = div6(i)
    src = r * 8 + (i - 6 * r) + first_col
    return jnp.where(iota((96, OWN), 1) == src, 1.0, 0.0).astype(BF16)


def corner_matrix(first_col):
    i = iota((80, 96), 0)
    second = i >= 40
    j = jnp.where(second, i - 40, i)
    r = div6(j)
    src = r * 8 + (j - 6 * r) + first_col + jnp.where(second, 48, 0)
    src = jnp.where(j < 36, src, -1)
    return jnp.where(iota((80, 96), 1) == src, 1.0, 0.0).astype(BF16)


def dot_t(a, b):
    return lax.dot_general(a, b, (((1,), (1,)), ((), ())), preferred_element_type=F32)


def dot(a, b):
    return jnp.dot(a, b, preferred_element_type=F32)


def kernel(n_lat, n_lon, pairs, q_hbm, k_hbm, v_hbm, c_hbm, o_hbm, dq_hbm, dk_hbm, dv_hbm,
           inputs, outputs, ext, snd_side, snd_corner, relay, bias1, bias2, perm, stat_acc, stat_mid, stat_side,
           stat_ext, in_sem, out_sem, side_s, side_r, corner_s, corner_r, strip_s, strip_r, relay_r, pass_s,
           stat_s, stat_r):
    lat, lon = lax.axis_index("lat"), lax.axis_index("lon")
    x = lax.rem(lat, XS)
    heads = 2 * pairs
    half = pairs // 2
    quarter = pairs // 4
    total_rows = n_lat * ROWS
    first = lat * ROWS
    scale = HEAD ** -0.5

    def device(a, b):
        return {"lat": lax.rem(lat + a + n_lat, n_lat), "lon": lax.rem(lon + b + n_lon, n_lon)}

    barrier = pltpu.get_barrier_semaphore()
    for a, b in GREETED:
        pl.semaphore_signal(barrier, inc=1, device_id=device(a, b), device_id_type=MESH)

    loads = [pltpu.make_async_copy(ref, inputs.at[i], in_sem.at[i])
             for i, ref in enumerate((k_hbm, v_hbm, q_hbm, c_hbm))]
    stores = [pltpu.make_async_copy(outputs.at[i], ref, out_sem.at[i])
              for i, ref in enumerate((o_hbm, dq_hbm, dk_hbm, dv_hbm))]
    for load in loads:
        load.start()

    def remote(src, dst, send, recv, to):
        return pltpu.make_async_remote_copy(
            src_ref=src, dst_ref=dst, send_sem=send, recv_sem=recv, device_id=to, device_id_type=MESH)

    def arrays(c):
        return pl.ds(2 * (c // 2), 2)

    def heads_of(c):
        return pl.ds(half * (c % 2), half)

    def from_to(c, d, which):
        at = heads_of(c) if which is None else pl.ds(half * (c % 2) + quarter * which, quarter)
        return (ext.at[arrays(c), at, pl.ds(80 if d == 0 else 0, 48)],
                ext.at[arrays(c), at, pl.ds(NN if d == 0 else SS, 48)])

    def strip(c, d, which=None):
        src, dst = from_to(c, d, which)
        return remote(src, dst, strip_s.at[c, d, 0], strip_r.at[c, d, 0], device(1 if d == 0 else -1, 0))

    def detour(c, d):
        src, _ = from_to(c, d, 1)
        return remote(src, relay.at[c, d], strip_s.at[c, d, 1], relay_r.at[c, d], device(4 if d == 0 else -4, 0))

    def passed(c, d):
        _, dst = from_to(c, d, 1)
        return remote(relay.at[c, d], dst, pass_s.at[c, d], strip_r.at[c, d, 1], device(-3 if d == 0 else 3, 0))

    last = (XS - 1, 0)

    def start_strips(c):
        for d in range(2):
            @pl.when(x != last[d])
            def _():
                strip(c, d).start()

            @pl.when(x == last[d])
            def _():
                detour(c, d).start()
                strip(c, d, 0).start()

    def pass_on(c):
        for d in range(2):
            @pl.when(x == last[d])
            def _():
                detour(c, d).wait_recv()
                passed(c, d).start()

    def wait_strips(c):
        for d in range(2):
            @pl.when(x != last[1 - d])
            def _():
                strip(c, d).wait_recv()

            @pl.when(x == last[1 - d])
            def _():
                strip(c, d, 0).wait_recv()
                passed(c, d).wait_recv()

    def sent_strips(c):
        for d in range(2):
            @pl.when(x != last[d])
            def _():
                strip(c, d).wait_send()

            @pl.when(x == last[d])
            def _():
                strip(c, d, 0).wait_send()
                detour(c, d).wait_send()
                passed(c, d).wait_send()

    def sides(c):
        return [remote(snd_side.at[i, arrays(c), heads_of(c)], ext.at[arrays(c), heads_of(c), pl.ds(to, 96)],
                       side_s.at[c, i], side_r.at[c, i], device(0, b))
                for i, (to, b) in enumerate(((WW, 1), (EE, -1)))]

    def corners(c):
        return [remote(snd_corner.at[i, arrays(c), heads_of(c)], ext.at[arrays(c), heads_of(c), pl.ds(to, 80)],
                       corner_s.at[c, i], corner_r.at[c, i], device(0, b))
                for i, (to, b) in enumerate(((WC, 1), (EC, -1)))]

    def start(copies):
        for copy in copies:
            copy.start()

    def arrived(copies):
        for copy in copies:
            copy.wait_recv()

    def pack(s):
        east, west = pack_matrix(2), pack_matrix(0)
        for a in (2 * s, 2 * s + 1):
            for p in range(pairs):
                block = inputs[a, :, 128 * p:128 * (p + 1)]
                ext[a, p, 0:OWN, :] = block
                snd_side[0, a, p] = dot(east, block).astype(BF16)
                snd_side[1, a, p] = dot(west, block).astype(BF16)

    def send_corners(c):
        wait_strips(c)
        east, west = corner_matrix(2), corner_matrix(0)
        for a in (2 * (c // 2), 2 * (c // 2) + 1):
            for p in range(half * (c % 2), half * (c % 2) + half):
                block = ext[a, p, NN:WW, :]
                snd_corner[0, a, p] = dot(east, block).astype(BF16)
                snd_corner[1, a, p] = dot(west, block).astype(BF16)
        start(corners(c))

    loads[0].wait()
    loads[1].wait()
    pack(0)
    pl.semaphore_wait(barrier, len(GREETED))
    for c in range(2):
        start_strips(c)
        start(sides(c))
    loads[2].wait()
    loads[3].wait()
    pack(1)

    row, col, ok = ext_coords(iota((8, EXT), 1))
    row, col, ok = row[0:1], col[0:1], jnp.where(ok, 1, 0)[0:1]
    token = iota((OWN, EXT), 0)
    near = (jnp.abs(col - (token & 7)) <= RADIUS) & (ok > 0)
    own_row = first + (token >> 3)
    ext_row = first + row
    begin = jnp.clip(own_row - RADIUS, 0, total_rows - 2 * RADIUS - 1)
    inside = near & (ext_row >= begin) & (ext_row <= begin + 2 * RADIUS)
    bias1[...] = jnp.where(inside, 0.0, NEG)
    begin = jnp.clip(ext_row - RADIUS, 0, total_rows - 2 * RADIUS - 1)
    inside = near & (own_row >= begin) & (own_row <= begin + 2 * RADIUS)
    inside = inside & (ext_row >= 0) & (ext_row < total_rows)
    bias2[...] = jnp.where(inside, 0.0, NEG)

    pass_on(0)
    pass_on(1)
    send_corners(0)
    send_corners(1)
    start_strips(2)
    start_strips(3)

    up, down = jnp.where(row < 0, -1, 0), jnp.where(row >= ROWS, 1, 0)
    left, right = jnp.where(col < 0, -3, 0), jnp.where(col >= COLS, 3, 0)
    src = (4 + up + down + left + right) * OWN + (row & (ROWS - 1)) * 8 + (col & (COLS - 1))
    src = jnp.where(ok > 0, src, -1)
    for b in range(9):
        at = iota((OWN, EXT), 0) + b * OWN
        perm[b * OWN:(b + 1) * OWN, :] = jnp.where(at == src, 1.0, 0.0).astype(BF16)

    lane = iota((1, 128), 1)
    lo = jnp.where(lane < HEAD, 1.0, 0.0).astype(BF16)
    hi = jnp.where(lane < HEAD, 0.0, 1.0).astype(BF16)
    lower = iota((OWN, 128), 1) < HEAD

    def by_head(v):
        return jnp.concatenate([v * lo, v * hi], axis=0)

    def merged(v):
        return jnp.where(lower, v[:OWN], v[OWN:])

    def lanes(p):
        return pl.ds(pl.multiple_of(p * 128, 128), 128)

    stat_acc[...] = jnp.zeros_like(stat_acc)

    def forward(p, carry):
        kx, vx = ext[0, p], ext[1, p]
        s = dot_t(by_head(ext[2, p, 0:OWN, :]), kx)
        dw = dot_t(by_head(ext[3, p, 0:OWN, :]), vx)
        acc = stat_acc[...]
        lane_at = iota((OWN, 128), 1)
        rounded, grads = [], []
        for h in range(2):
            of = slice(h * OWN, (h + 1) * OWN)
            t = s[of] * (scale * LOG2E) + bias1[...]
            m = jnp.max(t, axis=1, keepdims=True)
            e = jnp.exp2(t - m)
            total = jnp.sum(e, axis=1, keepdims=True)
            w = e * (1.0 / total)
            rounded.append(w.astype(BF16))
            g = dw[of]
            delta = jnp.sum(w * g, axis=1, keepdims=True)
            grads.append((w * (g - delta)).astype(BF16))
            acc = jnp.where(lane_at == 2 * p + h, m + jnp.log2(total), acc)
            acc = jnp.where(lane_at == heads + 2 * p + h, delta, acc)
        stat_acc[...] = acc
        o = dot(jnp.concatenate(rounded, axis=0), vx)
        dq = dot(jnp.concatenate(grads, axis=0), kx)
        outputs[0, :, lanes(p)] = merged(o).astype(BF16)
        outputs[1, :, lanes(p)] = (merged(dq) * scale).astype(BF16)
        return carry

    def backward(p, carry):
        qx, cx = ext[2, p], ext[3, p]
        s = dot_t(by_head(ext[0, p, 0:OWN, :]), qx)
        dw = dot_t(by_head(ext[1, p, 0:OWN, :]), cx)
        rounded, grads = [], []
        for h in range(2):
            of = slice(h * OWN, (h + 1) * OWN)
            norm = stat_ext[2 * p + h]
            delta = stat_ext[heads + 2 * p + h]
            w = jnp.exp2(s[of] * (scale * LOG2E) + bias2[...] - norm)
            rounded.append(w.astype(BF16))
            grads.append((w * (dw[of] - delta)).astype(BF16))
        dv = dot(jnp.concatenate(rounded, axis=0), cx)
        dk = dot(jnp.concatenate(grads, axis=0), qx)
        outputs[3, :, lanes(p)] = merged(dv).astype(BF16)
        outputs[2, :, lanes(p)] = (merged(dk) * scale).astype(BF16)
        return carry

    arrived(sides(0) + corners(0))
    start(sides(2))
    lax.fori_loop(0, half, forward, 0, unroll=2)
    start(sides(3))
    pass_on(2)
    pass_on(3)
    send_corners(2)
    send_corners(3)
    arrived(sides(1) + corners(1))
    lax.fori_loop(half, pairs, forward, 0, unroll=2)
    stores[0].start()
    stores[1].start()

    stat_mid[1] = stat_acc[...].T[0:2 * heads]
    stats = [remote(stat_mid.at[1], stat_mid.at[i], stat_s.at[k], stat_r.at[k], device(b, 0))
             for k, (i, b) in enumerate(((0, 1), (2, -1)))]
    around = [remote(stat_mid, stat_side.at[k], stat_s.at[2 + k], stat_r.at[2 + k], device(0, b))
              for k, b in enumerate((1, -1))]
    start(stats)
    arrived(stats)
    start(around)
    arrived(sides(2) + corners(2))
    arrived(around)
    whole = jnp.concatenate([stat_side[0, i] for i in range(3)] + [stat_mid[i] for i in range(3)]
                            + [stat_side[1, i] for i in range(3)], axis=1)
    x1 = whole.astype(BF16)
    rest = whole - x1.astype(F32)
    x2 = rest.astype(BF16)
    x3 = (rest - x2.astype(F32)).astype(BF16)
    y = dot(jnp.concatenate([x1, x2, x3], axis=0), perm[...])
    y = (y[0:2 * heads] + y[2 * heads:4 * heads]) + y[4 * heads:6 * heads]
    for i in range(2 * heads):
        stat_ext[i] = y[i:i + 1]

    lax.fori_loop(0, half, backward, 0, unroll=2)
    arrived(sides(3) + corners(3))
    lax.fori_loop(half, pairs, backward, 0, unroll=2)
    stores[2].start()
    stores[3].start()

    for c in range(4):
        sent_strips(c)
        for copy in sides(c) + corners(c):
            copy.wait_send()
    for copy in stats + around:
        copy.wait_send()
    for store in stores:
        store.wait()


def solution(mesh):
    n_lat, n_lon = mesh.shape["lat"], mesh.shape["lon"]

    def shards(queries, keys, values, cotangent):
        width = queries.shape[2]
        pairs = width // 128
        heads = 2 * pairs
        flat = [x.reshape(OWN, width) for x in (queries, keys, values, cotangent)]
        dma = pltpu.SemaphoreType.DMA
        outs = pl.pallas_call(
            functools.partial(kernel, n_lat, n_lon, pairs),
            out_shape=[jax.ShapeDtypeStruct((OWN, width), BF16)] * 4,
            in_specs=[pl.BlockSpec(memory_space=pltpu.HBM)] * 4,
            out_specs=[pl.BlockSpec(memory_space=pltpu.HBM)] * 4,
            scratch_shapes=[
                pltpu.VMEM((4, OWN, width), BF16),
                pltpu.VMEM((4, OWN, width), BF16),
                pltpu.VMEM((4, pairs, EXT, 128), BF16),
                pltpu.VMEM((2, 4, pairs, 96, 128), BF16),
                pltpu.VMEM((2, 4, pairs, 80, 128), BF16),
                pltpu.VMEM((4, 2, 2, pairs // 4, 48, 128), BF16),
                pltpu.VMEM((OWN, EXT), F32),
                pltpu.VMEM((OWN, EXT), F32),
                pltpu.VMEM((9 * OWN, EXT), BF16),
                pltpu.VMEM((OWN, 128), F32),
                pltpu.VMEM((3, 2 * heads, OWN), F32),
                pltpu.VMEM((2, 3, 2 * heads, OWN), F32),
                pltpu.VMEM((2 * heads, 1, EXT), F32),
                dma((4,)), dma((4,)), dma((4, 2)), dma((4, 2)), dma((4, 2)), dma((4, 2)),
                dma((4, 2, 2)), dma((4, 2, 2)), dma((4, 2)), dma((4, 2)), dma((4,)), dma((4,)),
            ],
            compiler_params=pltpu.CompilerParams(
                collective_id=0, has_side_effects=True, vmem_limit_bytes=63 * 1024 * 1024),
        )(*flat)
        return tuple(x.reshape(ROWS, COLS, width) for x in outs)

    spec = P("lat", "lon", None)
    return jax.shard_map(shards, mesh=mesh, in_specs=(spec,) * 4, out_specs=(spec,) * 4, check_vma=False)
```

```python
import functools

import jax
import jax.numpy as jnp
from jax import lax
from jax.experimental import pallas as pl
from jax.experimental.pallas import tpu as pltpu
from jax.sharding import PartitionSpec as P

RADIUS = 6
HEAD = 64
ROWS = 16
COLS = 8
OWN = ROWS * COLS
NN, SS, WW, EE, WC, EC, EXT = 128, 176, 224, 320, 416, 496, 576
SEGMENTS = [
    (0, 8, 0, 0, 128), (128, 8, -6, 0, 48), (176, 8, 16, 0, 48), (224, 6, 0, -6, 96), (320, 6, 0, 8, 96),
    (416, 6, -6, -6, 36), (456, 6, 16, -6, 36), (496, 6, -6, 8, 36), (536, 6, 16, 8, 36),
]
XS = 4
LOG2E = 1.4426950408889634
NEG = -1e30
F32, BF16, I32 = jnp.float32, jnp.bfloat16, jnp.int32
MESH = pl.DeviceIdType.MESH
GREETED = [(1, 0), (-1, 0), (4, 0), (-4, 0), (3, 0), (-3, 0), (0, 1), (0, -1)]
AROUND = [(a, b) for a in (-1, 0, 1) for b in (-1, 0, 1) if (a, b) != (0, 0)]


def iota(shape, dim):
    return lax.broadcasted_iota(I32, shape, dim)


def div6(x):
    return (x * 171) >> 10


def ext_coords(e):
    row = col = ok = None
    for first, wide, row0, col0, count in SEGMENTS:
        j = jnp.maximum(e - first, 0)
        r = (j >> 3) if wide == 8 else div6(j)
        c = j - wide * r + col0
        r = r + row0
        good = jnp.where(j < count, 1, 0)
        if row is None:
            row, col, ok = r, c, good
        else:
            row = jnp.where(e >= first, r, row)
            col = jnp.where(e >= first, c, col)
            ok = jnp.where(e >= first, good, ok)
    return row, col, ok > 0


def pack_matrix(first_col):
    i = iota((96, OWN), 0)
    r = div6(i)
    src = r * 8 + (i - 6 * r) + first_col
    return jnp.where(iota((96, OWN), 1) == src, 1.0, 0.0).astype(BF16)


def corner_matrix(first_col):
    i = iota((80, 96), 0)
    second = i >= 40
    j = jnp.where(second, i - 40, i)
    r = div6(j)
    src = r * 8 + (j - 6 * r) + first_col + jnp.where(second, 48, 0)
    src = jnp.where(j < 36, src, -1)
    return jnp.where(iota((80, 96), 1) == src, 1.0, 0.0).astype(BF16)


def dot_t(a, b):
    return lax.dot_general(a, b, (((1,), (1,)), ((), ())), preferred_element_type=F32)


def dot(a, b):
    return jnp.dot(a, b, preferred_element_type=F32)


def kernel(n_lat, n_lon, pairs, q_hbm, k_hbm, v_hbm, c_hbm, o_hbm, dq_hbm, dk_hbm, dv_hbm,
           inputs, outputs, ext, snd_side, snd_corner, relay, bias1, bias2, perm, stat_acc, stat_own, stat_in,
           stat_ext, in_sem, out_sem, side_s, side_r, corner_s, corner_r, strip_s, strip_r, relay_r, pass_s,
           stat_s, stat_r):
    lat, lon = lax.axis_index("lat"), lax.axis_index("lon")
    x = lax.rem(lat, XS)
    heads = 2 * pairs
    half = pairs // 2
    quarter = pairs // 4
    total_rows = n_lat * ROWS
    first = lat * ROWS
    scale = HEAD ** -0.5

    def device(a, b):
        return {"lat": lax.rem(lat + a + n_lat, n_lat), "lon": lax.rem(lon + b + n_lon, n_lon)}

    barrier = pltpu.get_barrier_semaphore()
    for a, b in GREETED:
        pl.semaphore_signal(barrier, inc=1, device_id=device(a, b), device_id_type=MESH)

    loads = [pltpu.make_async_copy(ref, inputs.at[i], in_sem.at[i])
             for i, ref in enumerate((k_hbm, v_hbm, q_hbm, c_hbm))]
    stores = [pltpu.make_async_copy(outputs.at[i], ref, out_sem.at[i])
              for i, ref in enumerate((o_hbm, dq_hbm, dk_hbm, dv_hbm))]
    for load in loads:
        load.start()

    def remote(src, dst, send, recv, to):
        return pltpu.make_async_remote_copy(
            src_ref=src, dst_ref=dst, send_sem=send, recv_sem=recv, device_id=to, device_id_type=MESH)

    def arrays(c):
        return pl.ds(2 * (c // 2), 2)

    def heads_of(c):
        return pl.ds(half * (c % 2), half)

    def from_to(c, d, which):
        at = heads_of(c) if which is None else pl.ds(half * (c % 2) + quarter * which, quarter)
        return (ext.at[arrays(c), at, pl.ds(80 if d == 0 else 0, 48)],
                ext.at[arrays(c), at, pl.ds(NN if d == 0 else SS, 48)])

    def strip(c, d, which=None):
        src, dst = from_to(c, d, which)
        return remote(src, dst, strip_s.at[c, d, 0], strip_r.at[c, d, 0], device(1 if d == 0 else -1, 0))

    def detour(c, d):
        src, _ = from_to(c, d, 1)
        return remote(src, relay.at[c, d], strip_s.at[c, d, 1], relay_r.at[c, d], device(-3 if d == 0 else 3, 0))

    def passed(c, d):
        _, dst = from_to(c, d, 1)
        return remote(relay.at[c, d], dst, pass_s.at[c, d], strip_r.at[c, d, 1], device(4 if d == 0 else -4, 0))

    last = (XS - 1, 0)

    def start_strips(c):
        for d in range(2):
            @pl.when(x != last[d])
            def _():
                strip(c, d).start()

            @pl.when(x == last[d])
            def _():
                strip(c, d, 0).start()

    def pass_on(c):
        for d in range(2):
            @pl.when(x == last[1 - d])
            def _():
                detour(c, d).wait_recv()
                passed(c, d).start()

    def wait_strips(c):
        for d in range(2):
            @pl.when(x != last[1 - d])
            def _():
                strip(c, d).wait_recv()

            @pl.when(x == last[1 - d])
            def _():
                strip(c, d, 0).wait_recv()
                passed(c, d).wait_recv()

    def sent_strips(c):
        for d in range(2):
            @pl.when(x != last[d])
            def _():
                strip(c, d).wait_send()

            @pl.when(x == last[d])
            def _():
                strip(c, d, 0).wait_send()
                detour(c, d).wait_send()

            @pl.when(x == last[1 - d])
            def _():
                passed(c, d).wait_send()

    def sides(c):
        return [remote(snd_side.at[i, arrays(c), heads_of(c)], ext.at[arrays(c), heads_of(c), pl.ds(to, 96)],
                       side_s.at[c, i], side_r.at[c, i], device(0, b))
                for i, (to, b) in enumerate(((WW, 1), (EE, -1)))]

    def corners(c):
        return [remote(snd_corner.at[i, arrays(c), heads_of(c)], ext.at[arrays(c), heads_of(c), pl.ds(to, 80)],
                       corner_s.at[c, i], corner_r.at[c, i], device(0, b))
                for i, (to, b) in enumerate(((WC, 1), (EC, -1)))]

    def start(copies):
        for copy in copies:
            copy.start()

    def arrived(copies):
        for copy in copies:
            copy.wait_recv()

    def pack(s):
        east, west = pack_matrix(2), pack_matrix(0)
        for a in (2 * s, 2 * s + 1):
            for p in range(pairs):
                block = inputs[a, :, 128 * p:128 * (p + 1)]
                ext[a, p, 0:OWN, :] = block
                snd_side[0, a, p] = dot(east, block).astype(BF16)
                snd_side[1, a, p] = dot(west, block).astype(BF16)

    def send_corners(c):
        wait_strips(c)
        east, west = corner_matrix(2), corner_matrix(0)
        for a in (2 * (c // 2), 2 * (c // 2) + 1):
            for p in range(half * (c % 2), half * (c % 2) + half):
                block = ext[a, p, NN:WW, :]
                snd_corner[0, a, p] = dot(east, block).astype(BF16)
                snd_corner[1, a, p] = dot(west, block).astype(BF16)
        start(corners(c))

    for load in loads:
        load.wait()
    pack(0)
    pack(1)
    pl.semaphore_wait(barrier, len(GREETED))
    for d in range(2):
        @pl.when(x == last[d])
        def _():
            for c in range(4):
                detour(c, d).start()
    for c in range(4):
        start_strips(c)
        if c < 3:
            start(sides(c))

    row, col, ok = ext_coords(iota((8, EXT), 1))
    row, col, ok = row[0:1], col[0:1], jnp.where(ok, 1, 0)[0:1]
    token = iota((OWN, EXT), 0)
    near = (jnp.abs(col - (token & 7)) <= RADIUS) & (ok > 0)
    own_row = first + (token >> 3)
    ext_row = first + row
    begin = jnp.clip(own_row - RADIUS, 0, total_rows - 2 * RADIUS - 1)
    inside = near & (ext_row >= begin) & (ext_row <= begin + 2 * RADIUS)
    bias1[...] = jnp.where(inside, 0.0, NEG)
    begin = jnp.clip(ext_row - RADIUS, 0, total_rows - 2 * RADIUS - 1)
    inside = near & (own_row >= begin) & (own_row <= begin + 2 * RADIUS)
    inside = inside & (ext_row >= 0) & (ext_row < total_rows)
    bias2[...] = jnp.where(inside, 0.0, NEG)

    up, down = jnp.where(row < 0, -3, 0), jnp.where(row >= ROWS, 3, 0)
    left, right = jnp.where(col < 0, -1, 0), jnp.where(col >= COLS, 1, 0)
    src = (4 + up + down + left + right) * OWN + (row & (ROWS - 1)) * 8 + (col & (COLS - 1))
    src = jnp.where(ok > 0, src, -1)
    for b in range(9):
        at = iota((OWN, EXT), 0) + b * OWN
        perm[b * OWN:(b + 1) * OWN, :] = jnp.where(at == src, 1.0, 0.0).astype(BF16)

    for c in range(4):
        pass_on(c)
    send_corners(0)
    send_corners(1)
    start(sides(3))

    lane = iota((1, 128), 1)
    lo = jnp.where(lane < HEAD, 1.0, 0.0).astype(BF16)
    hi = jnp.where(lane < HEAD, 0.0, 1.0).astype(BF16)
    lower = iota((OWN, 128), 1) < HEAD

    def by_head(v):
        return jnp.concatenate([v * lo, v * hi], axis=0)

    def merged(v):
        return jnp.where(lower, v[:OWN], v[OWN:])

    def lanes(p):
        return pl.ds(pl.multiple_of(p * 128, 128), 128)

    def forward(p, carry):
        kx, vx = ext[0, p], ext[1, p]
        s = dot_t(by_head(ext[2, p, 0:OWN, :]), kx)
        dw = dot_t(by_head(ext[3, p, 0:OWN, :]), vx)
        at = 2 * lax.rem(p, half)
        acc = stat_acc[...]
        lane_at = iota((OWN, 128), 1)
        rounded, grads = [], []
        for h in range(2):
            of = slice(h * OWN, (h + 1) * OWN)
            t = s[of] * (scale * LOG2E) + bias1[...]
            m = jnp.max(t, axis=1, keepdims=True)
            e = jnp.exp2(t - m)
            total = jnp.sum(e, axis=1, keepdims=True)
            w = e * (1.0 / total)
            rounded.append(w.astype(BF16))
            g = dw[of]
            delta = jnp.sum(w * g, axis=1, keepdims=True)
            grads.append((w * (g - delta)).astype(BF16))
            acc = jnp.where(lane_at == at + h, m + jnp.log2(total), acc)
            acc = jnp.where(lane_at == pairs + at + h, delta, acc)
        stat_acc[...] = acc
        o = dot(jnp.concatenate(rounded, axis=0), vx)
        dq = dot(jnp.concatenate(grads, axis=0), kx)
        outputs[0, :, lanes(p)] = merged(o).astype(BF16)
        outputs[1, :, lanes(p)] = (merged(dq) * scale).astype(BF16)
        return carry

    def backward(p, carry):
        qx, cx = ext[2, p], ext[3, p]
        s = dot_t(by_head(ext[0, p, 0:OWN, :]), qx)
        dw = dot_t(by_head(ext[1, p, 0:OWN, :]), cx)
        rounded, grads = [], []
        for h in range(2):
            of = slice(h * OWN, (h + 1) * OWN)
            norm = stat_ext[2 * p + h]
            delta = stat_ext[heads + 2 * p + h]
            w = jnp.exp2(s[of] * (scale * LOG2E) + bias2[...] - norm)
            rounded.append(w.astype(BF16))
            grads.append((w * (dw[of] - delta)).astype(BF16))
        dv = dot(jnp.concatenate(rounded, axis=0), cx)
        dk = dot(jnp.concatenate(grads, axis=0), qx)
        outputs[3, :, lanes(p)] = merged(dv).astype(BF16)
        outputs[2, :, lanes(p)] = (merged(dk) * scale).astype(BF16)
        return carry

    def stats(i):
        return [remote(stat_own.at[i], stat_in.at[i, n], stat_s.at[i, n], stat_r.at[i, n], device(-a, -b))
                for n, (a, b) in enumerate(AROUND)]

    def send_stats(i):
        stat_own[i] = stat_acc[...].T[0:heads]
        start(stats(i))

    def spread_stats(i):
        arrived(stats(i))
        whole = jnp.concatenate([stat_in[i, n] for n in range(4)] + [stat_own[i]]
                                + [stat_in[i, n] for n in range(4, 8)], axis=1)
        x1 = whole.astype(BF16)
        rest = whole - x1.astype(F32)
        x2 = rest.astype(BF16)
        x3 = (rest - x2.astype(F32)).astype(BF16)
        y = dot(jnp.concatenate([x1, x2, x3], axis=0), perm[...])
        y = (y[0:heads] + y[heads:2 * heads]) + y[2 * heads:3 * heads]
        for k in range(pairs):
            stat_ext[pairs * i + k] = y[k:k + 1]
            stat_ext[heads + pairs * i + k] = y[pairs + k:pairs + k + 1]

    stat_acc[...] = jnp.zeros_like(stat_acc)
    arrived(sides(0) + corners(0))
    send_corners(2)
    lax.fori_loop(0, half, forward, 0, unroll=2)
    send_stats(0)
    send_corners(3)
    arrived(sides(1) + corners(1))
    lax.fori_loop(half, pairs, forward, 0, unroll=2)
    send_stats(1)
    stores[0].start()
    stores[1].start()
    spread_stats(0)
    arrived(sides(2) + corners(2))
    lax.fori_loop(0, half, backward, 0, unroll=2)
    spread_stats(1)
    arrived(sides(3) + corners(3))
    lax.fori_loop(half, pairs, backward, 0, unroll=2)
    stores[2].start()
    stores[3].start()

    for c in range(4):
        sent_strips(c)
        for copy in sides(c) + corners(c):
            copy.wait_send()
    for i in range(2):
        for copy in stats(i):
            copy.wait_send()
    for store in stores:
        store.wait()


def solution(mesh):
    n_lat, n_lon = mesh.shape["lat"], mesh.shape["lon"]

    def shards(queries, keys, values, cotangent):
        width = queries.shape[2]
        pairs = width // 128
        heads = 2 * pairs
        flat = [x.reshape(OWN, width) for x in (queries, keys, values, cotangent)]
        dma = pltpu.SemaphoreType.DMA
        outs = pl.pallas_call(
            functools.partial(kernel, n_lat, n_lon, pairs),
            out_shape=[jax.ShapeDtypeStruct((OWN, width), BF16)] * 4,
            in_specs=[pl.BlockSpec(memory_space=pltpu.HBM)] * 4,
            out_specs=[pl.BlockSpec(memory_space=pltpu.HBM)] * 4,
            scratch_shapes=[
                pltpu.VMEM((4, OWN, width), BF16),
                pltpu.VMEM((4, OWN, width), BF16),
                pltpu.VMEM((4, pairs, EXT, 128), BF16),
                pltpu.VMEM((2, 4, pairs, 96, 128), BF16),
                pltpu.VMEM((2, 4, pairs, 80, 128), BF16),
                pltpu.VMEM((4, 2, 2, pairs // 4, 48, 128), BF16),
                pltpu.VMEM((OWN, EXT), F32),
                pltpu.VMEM((OWN, EXT), F32),
                pltpu.VMEM((9 * OWN, EXT), BF16),
                pltpu.VMEM((OWN, 128), F32),
                pltpu.VMEM((2, heads, OWN), F32),
                pltpu.VMEM((2, 8, heads, OWN), F32),
                pltpu.VMEM((2 * heads, 1, EXT), F32),
                dma((4,)), dma((4,)), dma((4, 2)), dma((4, 2)), dma((4, 2)), dma((4, 2)),
                dma((4, 2, 2)), dma((4, 2, 2)), dma((4, 2)), dma((4, 2)), dma((2, 8)), dma((2, 8)),
            ],
            compiler_params=pltpu.CompilerParams(
                collective_id=0, has_side_effects=True, vmem_limit_bytes=63 * 1024 * 1024),
        )(*flat)
        return tuple(x.reshape(ROWS, COLS, width) for x in outs)

    spec = P("lat", "lon", None)
    return jax.shard_map(shards, mesh=mesh, in_specs=(spec,) * 4, out_specs=(spec,) * 4, check_vma=False)
```

```python
import functools

import jax
import jax.numpy as jnp
from jax import lax
from jax.experimental import pallas as pl
from jax.experimental.pallas import tpu as pltpu
from jax.sharding import PartitionSpec as P

RADIUS = 6
HEAD = 64
ROWS = 16
COLS = 8
OWN = ROWS * COLS
NN, SS, WW, EE, WC, EC, EXT = 128, 176, 224, 320, 416, 512, 608
SEGMENTS = [
    (0, 8, 0, 0, 128), (128, 8, -6, 0, 48), (176, 8, 16, 0, 48), (224, 6, 0, -6, 96), (320, 6, 0, 8, 96),
    (416, 6, -8, -6, 48), (464, 6, 16, -6, 48), (512, 6, -8, 8, 48), (560, 6, 16, 8, 48),
]
XS = 4
LOG2E = 1.4426950408889634
NEG = -1e30
F32, BF16, I32 = jnp.float32, jnp.bfloat16, jnp.int32
MESH = pl.DeviceIdType.MESH
GREETED = [(a, 0) for a in (-4, -3, -2, -1, 1, 2, 3, 4)] + [(0, 1), (0, -1)]
FOUR, TWO = [(0, 0, 1), (1, 1, 1), (2, 2, 1), (3, 3, 1)], [(0, 0, 2), (3, 2, 2)]
AROUND = [(a, b) for a in (-1, 0, 1) for b in (-1, 0, 1) if (a, b) != (0, 0)]


def iota(shape, dim):
    return lax.broadcasted_iota(I32, shape, dim)


def div6(x):
    return (x * 171) >> 10


def ext_coords(e):
    row = col = ok = None
    for first, wide, row0, col0, count in SEGMENTS:
        j = jnp.maximum(e - first, 0)
        r = (j >> 3) if wide == 8 else div6(j)
        c = j - wide * r + col0
        r = r + row0
        good = jnp.where(j < count, 1, 0)
        if row is None:
            row, col, ok = r, c, good
        else:
            row = jnp.where(e >= first, r, row)
            col = jnp.where(e >= first, c, col)
            ok = jnp.where(e >= first, good, ok)
    return row, col, ok > 0


def pack_matrix(first_col):
    i = iota((96, OWN), 0)
    r = div6(i)
    src = r * 8 + (i - 6 * r) + first_col
    return jnp.where(iota((96, OWN), 1) == src, 1.0, 0.0).astype(BF16)


def corner_matrix(first_col):
    i = iota((96, 96), 0)
    r = div6(i)
    src = (r - 2) * 8 + (i - 6 * r) + first_col
    src = jnp.where((i >= 12) & (i < 84), src, -1)
    return jnp.where(iota((96, 96), 1) == src, 1.0, 0.0).astype(BF16)


def dot_t(a, b):
    return lax.dot_general(a, b, (((1,), (1,)), ((), ())), preferred_element_type=F32)


def dot(a, b):
    return jnp.dot(a, b, preferred_element_type=F32)


def kernel(n_lat, n_lon, pairs, q_hbm, k_hbm, v_hbm, c_hbm, o_hbm, dq_hbm, dk_hbm, dv_hbm,
           inputs, outputs, ext, snd_side, snd_corner, relay, bias1, bias2, perm, stat_acc, stat_own, stat_in,
           stat_ext, in_sem, out_sem, side_s, side_r, corner_s, corner_r, cut_s, strip_s, strip_r, relay_r, pass_s,
           stat_s, stat_r):
    lat, lon = lax.axis_index("lat"), lax.axis_index("lon")
    x = lax.rem(lat, XS)
    heads = 2 * pairs
    half = pairs // 2
    ring = min(16, n_lon)
    total_rows = n_lat * ROWS
    first = lat * ROWS
    scale = HEAD ** -0.5

    def device(a, b):
        return {"lat": lax.rem(lat + a + n_lat, n_lat), "lon": lax.rem(lon + b + n_lon, n_lon)}

    barrier = pltpu.get_barrier_semaphore()
    for a, b in GREETED:
        pl.semaphore_signal(barrier, inc=1, device_id=device(a, b), device_id_type=MESH)

    loads = [pltpu.make_async_copy(ref, inputs.at[i], in_sem.at[i])
             for i, ref in enumerate((k_hbm, v_hbm, q_hbm, c_hbm))]
    stores = [pltpu.make_async_copy(outputs.at[i], ref, out_sem.at[i])
              for i, ref in enumerate((o_hbm, dq_hbm, dk_hbm, dv_hbm))]
    for load in loads:
        load.start()

    def remote(src, dst, send, recv, to):
        return pltpu.make_async_remote_copy(
            src_ref=src, dst_ref=dst, send_sem=send, recv_sem=recv, device_id=to, device_id_type=MESH)

    def arrays(c):
        return pl.ds(2 * (c // 2), 2)

    def heads_of(c):
        return pl.ds(half * (c % 2), half)

    def from_to(c, d, lo, n):
        at = pl.ds(half * (c % 2) + lo, n)
        return (ext.at[arrays(c), at, pl.ds(80 if d == 0 else 0, 48)],
                ext.at[arrays(c), at, pl.ds(NN if d == 0 else SS, 48)])

    last = (XS - 1, 0)
    edge = lax.rem(lon, ring)
    at_wrap = (edge < 2) | (edge >= ring - 2)
    plans = [(FOUR, at_wrap), (TWO, jnp.logical_not(at_wrap))]

    def strip(c, d):
        src, dst = from_to(c, d, 0, half)
        return remote(src, dst, strip_s.at[c, d, 0], strip_r.at[c, d, 0], device(1 if d == 0 else -1, 0))

    def part(c, d, j, lo, n):
        src, dst = from_to(c, d, lo, n)
        if j == last[d]:
            return remote(src, dst, strip_s.at[c, d, j], strip_r.at[c, d, j], device(1 if d == 0 else -1, 0))
        return remote(src, relay.at[c, d, :, pl.ds(0, n)], strip_s.at[c, d, j], relay_r.at[c, d],
                      device(j - XS + 1 if d == 0 else j, 0))

    def passed(c, d, j, lo, n):
        _, dst = from_to(c, d, lo, n)
        return remote(relay.at[c, d, :, pl.ds(0, n)], dst, pass_s.at[c, d], strip_r.at[c, d, j],
                      device(XS - j if d == 0 else -1 - j, 0))

    def start_detours():
        for plan, here in plans:
            for d in range(2):
                @pl.when(here & (x == last[d]))
                def _():
                    for c in range(4):
                        for j, lo, n in plan:
                            if j != last[d]:
                                part(c, d, j, lo, n).start()

    def start_strips(c):
        for d in range(2):
            @pl.when(x != last[d])
            def _():
                strip(c, d).start()

            for plan, here in plans:
                @pl.when(here & (x == last[d]))
                def _():
                    for j, lo, n in plan:
                        if j == last[d]:
                            part(c, d, j, lo, n).start()

    def pass_on(c):
        for plan, here in plans:
            for d in range(2):
                for j, lo, n in plan:
                    if j != last[d]:
                        @pl.when(here & (x == j))
                        def _():
                            part(c, d, j, lo, n).wait_recv()
                            passed(c, d, j, lo, n).start()

    def wait_strips(c):
        for d in range(2):
            @pl.when(x != last[1 - d])
            def _():
                strip(c, d).wait_recv()

            for plan, here in plans:
                @pl.when(here & (x == last[1 - d]))
                def _():
                    for j, lo, n in plan:
                        passed(c, d, j, lo, n).wait_recv()

    def sent_strips(c):
        for d in range(2):
            @pl.when(x != last[d])
            def _():
                strip(c, d).wait_send()

            for plan, here in plans:
                @pl.when(here & (x == last[d]))
                def _():
                    for j, lo, n in plan:
                        part(c, d, j, lo, n).wait_send()

                for j, lo, n in plan:
                    if j != last[d]:
                        @pl.when(here & (x == j))
                        def _():
                            passed(c, d, j, lo, n).wait_send()

    def sides(c):
        return [remote(snd_side.at[i, arrays(c), heads_of(c)], ext.at[arrays(c), heads_of(c), pl.ds(to, 96)],
                       side_s.at[c, i], side_r.at[c, i], device(0, b))
                for i, (to, b) in enumerate(((WW, 1), (EE, -1)))]

    wraps = (edge == 0, edge == ring - 1)
    poles = (x == 0, x == XS - 1)

    def corner(c, i, k):
        at = (arrays(c), heads_of(c))
        return remote(snd_corner.at[i, *at, pl.ds(48 * k, 48)], ext.at[*at, pl.ds((WC, EC)[i] + 48 * k, 48)],
                      corner_s.at[c, i, k], corner_r.at[c, i, k], device(0, 1 - 2 * i))

    def cut(c, i, k):
        at = (arrays(c), heads_of(c))
        return remote(ext.at[*at, pl.ds((WW, EE)[i] + 48 * (1 - k), 48)], ext.at[*at, pl.ds((WC, EC)[i] + 48 * k, 48)],
                      cut_s.at[c, i, k], corner_r.at[c, i, k], device(1 - 2 * k, 0))

    def each_corner(c, do):
        for i in range(2):
            for k in range(2):
                @pl.when(jnp.logical_not(wraps[1 - i]) | poles[k])
                def _():
                    do(corner(c, i, k))

    def each_cut(c, do):
        for i in range(2):
            for k in range(2):
                @pl.when(wraps[i] & jnp.logical_not(poles[1 - k]))
                def _():
                    do(cut(c, i, k))

    def wait_corners(c):
        for i in range(2):
            for k in range(2):
                corner(c, i, k).wait_recv()

    def start(copies):
        for copy in copies:
            copy.start()

    def arrived(copies):
        for copy in copies:
            copy.wait_recv()

    def pack(s):
        east, west = pack_matrix(2), pack_matrix(0)
        for a in (2 * s, 2 * s + 1):
            for p in range(pairs):
                block = inputs[a, :, 128 * p:128 * (p + 1)]
                ext[a, p, 0:OWN, :] = block
                snd_side[0, a, p] = dot(east, block).astype(BF16)
                snd_side[1, a, p] = dot(west, block).astype(BF16)

    def send_corners(c):
        wait_strips(c)
        east, west = corner_matrix(2), corner_matrix(0)
        for a in (2 * (c // 2), 2 * (c // 2) + 1):
            for p in range(half * (c % 2), half * (c % 2) + half):
                block = ext[a, p, NN:WW, :]
                snd_corner[0, a, p] = dot(east, block).astype(BF16)
                snd_corner[1, a, p] = dot(west, block).astype(BF16)
        each_corner(c, lambda copy: copy.start())

    def land_sides(c):
        arrived(sides(c))
        each_cut(c, lambda copy: copy.start())

    for load in loads:
        load.wait()
    pack(0)
    pack(1)
    pl.semaphore_wait(barrier, len(GREETED))
    start_detours()
    start_strips(0)
    start_strips(1)
    start(sides(0))
    row, col, ok = ext_coords(iota((8, EXT), 1))
    row, col, ok = row[0:1], col[0:1], jnp.where(ok, 1, 0)[0:1]
    token = iota((OWN, EXT), 0)
    near = (jnp.abs(col - (token & 7)) <= RADIUS) & (ok > 0)
    own_row = first + (token >> 3)
    ext_row = first + row
    begin = jnp.clip(own_row - RADIUS, 0, total_rows - 2 * RADIUS - 1)
    inside = near & (ext_row >= begin) & (ext_row <= begin + 2 * RADIUS)
    bias1[...] = jnp.where(inside, 0.0, NEG)
    begin = jnp.clip(ext_row - RADIUS, 0, total_rows - 2 * RADIUS - 1)
    inside = near & (own_row >= begin) & (own_row <= begin + 2 * RADIUS)
    inside = inside & (ext_row >= 0) & (ext_row < total_rows)
    bias2[...] = jnp.where(inside, 0.0, NEG)

    up, down = jnp.where(row < 0, -3, 0), jnp.where(row >= ROWS, 3, 0)
    left, right = jnp.where(col < 0, -1, 0), jnp.where(col >= COLS, 1, 0)
    src = (4 + up + down + left + right) * OWN + (row & (ROWS - 1)) * 8 + (col & (COLS - 1))
    src = jnp.where(ok > 0, src, -1)
    for b in range(9):
        at = iota((OWN, EXT), 0) + b * OWN
        perm[b * OWN:(b + 1) * OWN, :] = jnp.where(at == src, 1.0, 0.0).astype(BF16)

    pass_on(0)
    pass_on(1)
    start(sides(1))
    start_strips(2)
    start_strips(3)
    pass_on(2)
    pass_on(3)
    start(sides(2))
    send_corners(0)
    send_corners(1)
    start(sides(3))
    land_sides(0)
    land_sides(1)
    land_sides(2)
    send_corners(2)
    lane = iota((1, 128), 1)
    lo = jnp.where(lane < HEAD, 1.0, 0.0).astype(BF16)
    hi = jnp.where(lane < HEAD, 0.0, 1.0).astype(BF16)
    lower = iota((OWN, 128), 1) < HEAD

    def by_head(v):
        return jnp.concatenate([v * lo, v * hi], axis=0)

    def merged(v):
        return jnp.where(lower, v[:OWN], v[OWN:])

    def lanes(p):
        return pl.ds(pl.multiple_of(p * 128, 128), 128)

    def forward(p, carry):
        kx, vx = ext[0, p], ext[1, p]
        s = dot_t(by_head(ext[2, p, 0:OWN, :]), kx)
        dw = dot_t(by_head(ext[3, p, 0:OWN, :]), vx)
        at = 2 * lax.rem(p, half)
        acc = stat_acc[...]
        lane_at = iota((OWN, 128), 1)
        rounded, grads = [], []
        for h in range(2):
            of = slice(h * OWN, (h + 1) * OWN)
            t = s[of] * (scale * LOG2E) + bias1[...]
            m = jnp.max(t, axis=1, keepdims=True)
            e = jnp.exp2(t - m)
            total = jnp.sum(e, axis=1, keepdims=True)
            w = e * (1.0 / total)
            rounded.append(w.astype(BF16))
            g = dw[of]
            delta = jnp.sum(w * g, axis=1, keepdims=True)
            grads.append((w * (g - delta)).astype(BF16))
            acc = jnp.where(lane_at == at + h, m + jnp.log2(total), acc)
            acc = jnp.where(lane_at == pairs + at + h, delta, acc)
        stat_acc[...] = acc
        o = dot(jnp.concatenate(rounded, axis=0), vx)
        dq = dot(jnp.concatenate(grads, axis=0), kx)
        outputs[0, :, lanes(p)] = merged(o).astype(BF16)
        outputs[1, :, lanes(p)] = (merged(dq) * scale).astype(BF16)
        return carry

    def backward(p, carry):
        qx, cx = ext[2, p], ext[3, p]
        s = dot_t(by_head(ext[0, p, 0:OWN, :]), qx)
        dw = dot_t(by_head(ext[1, p, 0:OWN, :]), cx)
        rounded, grads = [], []
        for h in range(2):
            of = slice(h * OWN, (h + 1) * OWN)
            norm = stat_ext[2 * p + h]
            delta = stat_ext[heads + 2 * p + h]
            w = jnp.exp2(s[of] * (scale * LOG2E) + bias2[...] - norm)
            rounded.append(w.astype(BF16))
            grads.append((w * (dw[of] - delta)).astype(BF16))
        dv = dot(jnp.concatenate(rounded, axis=0), cx)
        dk = dot(jnp.concatenate(grads, axis=0), qx)
        outputs[3, :, lanes(p)] = merged(dv).astype(BF16)
        outputs[2, :, lanes(p)] = (merged(dk) * scale).astype(BF16)
        return carry

    def stats(i):
        return [remote(stat_own.at[i], stat_in.at[i, n], stat_s.at[i, n], stat_r.at[i, n], device(-a, -b))
                for n, (a, b) in enumerate(AROUND)]

    def send_stats(i):
        stat_own[i] = stat_acc[...].T[0:heads]
        start(stats(i))

    def spread_stats(i):
        arrived(stats(i))
        whole = jnp.concatenate([stat_in[i, n] for n in range(4)] + [stat_own[i]]
                                + [stat_in[i, n] for n in range(4, 8)], axis=1)
        x1 = whole.astype(BF16)
        rest = whole - x1.astype(F32)
        x2 = rest.astype(BF16)
        x3 = (rest - x2.astype(F32)).astype(BF16)
        y = dot(jnp.concatenate([x1, x2, x3], axis=0), perm[...])
        y = (y[0:heads] + y[heads:2 * heads]) + y[2 * heads:3 * heads]
        for k in range(pairs):
            stat_ext[pairs * i + k] = y[k:k + 1]
            stat_ext[heads + pairs * i + k] = y[pairs + k:pairs + k + 1]

    stat_acc[...] = jnp.zeros_like(stat_acc)
    wait_corners(0)
    lax.fori_loop(0, half, forward, 0, unroll=4)
    send_stats(0)
    land_sides(3)
    send_corners(3)
    wait_corners(1)
    lax.fori_loop(half, pairs, forward, 0, unroll=4)
    send_stats(1)
    stores[0].start()
    stores[1].start()
    spread_stats(0)
    wait_corners(2)
    lax.fori_loop(0, half, backward, 0, unroll=4)
    spread_stats(1)
    wait_corners(3)
    lax.fori_loop(half, pairs, backward, 0, unroll=4)
    stores[2].start()
    stores[3].start()

    for c in range(4):
        sent_strips(c)
        each_corner(c, lambda copy: copy.wait_send())
        each_cut(c, lambda copy: copy.wait_send())
        for copy in sides(c):
            copy.wait_send()
    for i in range(2):
        for copy in stats(i):
            copy.wait_send()
    for store in stores:
        store.wait()


def solution(mesh):
    n_lat, n_lon = mesh.shape["lat"], mesh.shape["lon"]

    def shards(queries, keys, values, cotangent):
        width = queries.shape[2]
        pairs = width // 128
        heads = 2 * pairs
        flat = [x.reshape(OWN, width) for x in (queries, keys, values, cotangent)]
        dma = pltpu.SemaphoreType.DMA
        outs = pl.pallas_call(
            functools.partial(kernel, n_lat, n_lon, pairs),
            out_shape=[jax.ShapeDtypeStruct((OWN, width), BF16)] * 4,
            in_specs=[pl.BlockSpec(memory_space=pltpu.HBM)] * 4,
            out_specs=[pl.BlockSpec(memory_space=pltpu.HBM)] * 4,
            scratch_shapes=[
                pltpu.VMEM((4, OWN, width), BF16),
                pltpu.VMEM((4, OWN, width), BF16),
                pltpu.VMEM((4, pairs, EXT, 128), BF16),
                pltpu.VMEM((2, 4, pairs, 96, 128), BF16),
                pltpu.VMEM((2, 4, pairs, 96, 128), BF16),
                pltpu.VMEM((4, 2, 2, 2, 48, 128), BF16),
                pltpu.VMEM((OWN, EXT), F32),
                pltpu.VMEM((OWN, EXT), F32),
                pltpu.VMEM((9 * OWN, EXT), BF16),
                pltpu.VMEM((OWN, 128), F32),
                pltpu.VMEM((2, heads, OWN), F32),
                pltpu.VMEM((2, 8, heads, OWN), F32),
                pltpu.VMEM((2 * heads, 1, EXT), F32),
                dma((4,)), dma((4,)), dma((4, 2)), dma((4, 2)), dma((4, 2, 2)), dma((4, 2, 2)), dma((4, 2, 2)),
                dma((4, 2, XS)), dma((4, 2, XS)), dma((4, 2)), dma((4, 2)), dma((2, 8)), dma((2, 8)),
            ],
            compiler_params=pltpu.CompilerParams(
                collective_id=0, has_side_effects=True, vmem_limit_bytes=63 * 1024 * 1024),
        )(*flat)
        return tuple(x.reshape(ROWS, COLS, width) for x in outs)

    spec = P("lat", "lon", None)
    return jax.shard_map(shards, mesh=mesh, in_specs=(spec,) * 4, out_specs=(spec,) * 4, check_vma=False)
```

```python
import functools

import jax
import jax.numpy as jnp
from jax import lax
from jax.experimental import pallas as pl
from jax.experimental.pallas import tpu as pltpu
from jax.sharding import PartitionSpec as P

RADIUS = 6
HEAD = 64
ROWS = 16
COLS = 8
OWN = ROWS * COLS
NN, SS, WW, EE, WC, EC, EXT = 128, 176, 224, 320, 416, 512, 608
SEGMENTS = [
    (0, 8, 0, 0, 128), (128, 8, -6, 0, 48), (176, 8, 16, 0, 48), (224, 6, 0, -6, 96), (320, 6, 0, 8, 96),
    (416, 6, -8, -6, 48), (464, 6, 16, -6, 48), (512, 6, -8, 8, 48), (560, 6, 16, 8, 48),
]
XS = 4
LOG2E = 1.4426950408889634
NEG = -1e30
F32, BF16, I32 = jnp.float32, jnp.bfloat16, jnp.int32
MESH = pl.DeviceIdType.MESH
GREETED = [(a, 0) for a in (-4, -3, -2, -1, 1, 2, 3, 4)] + [(0, 1), (0, -1)]
FOUR, TWO = [(0, 0, 1), (1, 1, 1), (2, 2, 1), (3, 3, 1)], [(0, 0, 2), (3, 2, 2)]
AROUND = [(a, b) for a in (-1, 0, 1) for b in (-1, 0, 1) if (a, b) != (0, 0)]


def iota(shape, dim):
    return lax.broadcasted_iota(I32, shape, dim)


def div6(x):
    return (x * 171) >> 10


def ext_coords(e):
    row = col = ok = None
    for first, wide, row0, col0, count in SEGMENTS:
        j = jnp.maximum(e - first, 0)
        r = (j >> 3) if wide == 8 else div6(j)
        c = j - wide * r + col0
        r = r + row0
        good = jnp.where(j < count, 1, 0)
        if row is None:
            row, col, ok = r, c, good
        else:
            row = jnp.where(e >= first, r, row)
            col = jnp.where(e >= first, c, col)
            ok = jnp.where(e >= first, good, ok)
    return row, col, ok > 0


def pack_matrix(first_col):
    i = iota((96, OWN), 0)
    r = div6(i)
    src = r * 8 + (i - 6 * r) + first_col
    return jnp.where(iota((96, OWN), 1) == src, 1.0, 0.0).astype(BF16)


def corner_matrix(first_col):
    i = iota((96, 96), 0)
    r = div6(i)
    src = (r - 2) * 8 + (i - 6 * r) + first_col
    src = jnp.where((i >= 12) & (i < 84), src, -1)
    return jnp.where(iota((96, 96), 1) == src, 1.0, 0.0).astype(BF16)


def dot_t(a, b):
    return lax.dot_general(a, b, (((1,), (1,)), ((), ())), preferred_element_type=F32)


def dot(a, b):
    return jnp.dot(a, b, preferred_element_type=F32)


def kernel(n_lat, n_lon, pairs, q_hbm, k_hbm, v_hbm, c_hbm, outputs,
           inputs, ext, snd_side, snd_corner, relay, bias1, bias2, perm, stat_acc, stat_own, stat_in,
           stat_ext, in_sem, side_s, side_r, corner_s, corner_r, cut_s, strip_s, strip_r, relay_r, pass_s,
           stat_s, stat_r):
    lat, lon = lax.axis_index("lat"), lax.axis_index("lon")
    x = lax.rem(lat, XS)
    heads = 2 * pairs
    half = pairs // 2
    ring = min(16, n_lon)
    total_rows = n_lat * ROWS
    first = lat * ROWS
    scale = HEAD ** -0.5

    def device(a, b):
        return {"lat": lax.rem(lat + a + n_lat, n_lat), "lon": lax.rem(lon + b + n_lon, n_lon)}

    barrier = pltpu.get_barrier_semaphore()
    for a, b in GREETED:
        pl.semaphore_signal(barrier, inc=1, device_id=device(a, b), device_id_type=MESH)

    loads = [pltpu.make_async_copy(ref, inputs.at[i], in_sem.at[i])
             for i, ref in enumerate((k_hbm, v_hbm, q_hbm, c_hbm))]
    for load in loads:
        load.start()

    def remote(src, dst, send, recv, to):
        return pltpu.make_async_remote_copy(
            src_ref=src, dst_ref=dst, send_sem=send, recv_sem=recv, device_id=to, device_id_type=MESH)

    def arrays(c):
        return pl.ds(2 * (c // 2), 2)

    def heads_of(c):
        return pl.ds(half * (c % 2), half)

    def from_to(c, d, lo, n):
        at = pl.ds(half * (c % 2) + lo, n)
        return (ext.at[arrays(c), at, pl.ds(80 if d == 0 else 0, 48)],
                ext.at[arrays(c), at, pl.ds(NN if d == 0 else SS, 48)])

    last = (XS - 1, 0)
    edge = lax.rem(lon, ring)
    at_wrap = (edge < 2) | (edge >= ring - 2)
    plans = [(FOUR, at_wrap), (TWO, jnp.logical_not(at_wrap))]

    def strip(c, d):
        src, dst = from_to(c, d, 0, half)
        return remote(src, dst, strip_s.at[c, d, 0], strip_r.at[c, d, 0], device(1 if d == 0 else -1, 0))

    def part(c, d, j, lo, n):
        src, dst = from_to(c, d, lo, n)
        if j == last[d]:
            return remote(src, dst, strip_s.at[c, d, j], strip_r.at[c, d, j], device(1 if d == 0 else -1, 0))
        return remote(src, relay.at[c, d, :, pl.ds(0, n)], strip_s.at[c, d, j], relay_r.at[c, d],
                      device(j - XS + 1 if d == 0 else j, 0))

    def passed(c, d, j, lo, n):
        _, dst = from_to(c, d, lo, n)
        return remote(relay.at[c, d, :, pl.ds(0, n)], dst, pass_s.at[c, d], strip_r.at[c, d, j],
                      device(XS - j if d == 0 else -1 - j, 0))

    def start_detours():
        for plan, here in plans:
            for d in range(2):
                @pl.when(here & (x == last[d]))
                def _():
                    for c in range(4):
                        for j, lo, n in plan:
                            if j != last[d]:
                                part(c, d, j, lo, n).start()

    def start_strips(c):
        for d in range(2):
            @pl.when(x != last[d])
            def _():
                strip(c, d).start()

            for plan, here in plans:
                @pl.when(here & (x == last[d]))
                def _():
                    for j, lo, n in plan:
                        if j == last[d]:
                            part(c, d, j, lo, n).start()

    def pass_on(c):
        for plan, here in plans:
            for d in range(2):
                for j, lo, n in plan:
                    if j != last[d]:
                        @pl.when(here & (x == j))
                        def _():
                            part(c, d, j, lo, n).wait_recv()
                            passed(c, d, j, lo, n).start()

    def wait_strips(c):
        for d in range(2):
            @pl.when(x != last[1 - d])
            def _():
                strip(c, d).wait_recv()

            for plan, here in plans:
                @pl.when(here & (x == last[1 - d]))
                def _():
                    for j, lo, n in plan:
                        passed(c, d, j, lo, n).wait_recv()

    def sent_strips(c):
        for d in range(2):
            @pl.when(x != last[d])
            def _():
                strip(c, d).wait_send()

            for plan, here in plans:
                @pl.when(here & (x == last[d]))
                def _():
                    for j, lo, n in plan:
                        part(c, d, j, lo, n).wait_send()

                for j, lo, n in plan:
                    if j != last[d]:
                        @pl.when(here & (x == j))
                        def _():
                            passed(c, d, j, lo, n).wait_send()

    def sides(c):
        return [remote(snd_side.at[i, arrays(c), heads_of(c)], ext.at[arrays(c), heads_of(c), pl.ds(to, 96)],
                       side_s.at[c, i], side_r.at[c, i], device(0, b))
                for i, (to, b) in enumerate(((WW, 1), (EE, -1)))]

    wraps = (edge == 0, edge == ring - 1)
    poles = (x == 0, x == XS - 1)

    def corner(c, i, k):
        at = (arrays(c), heads_of(c))
        return remote(snd_corner.at[i, *at, pl.ds(48 * k, 48)], ext.at[*at, pl.ds((WC, EC)[i] + 48 * k, 48)],
                      corner_s.at[c, i, k], corner_r.at[c, i, k], device(0, 1 - 2 * i))

    def cut(c, i, k):
        at = (arrays(c), heads_of(c))
        return remote(ext.at[*at, pl.ds((WW, EE)[i] + 48 * (1 - k), 48)], ext.at[*at, pl.ds((WC, EC)[i] + 48 * k, 48)],
                      cut_s.at[c, i, k], corner_r.at[c, i, k], device(1 - 2 * k, 0))

    def each_corner(c, do):
        for i in range(2):
            for k in range(2):
                @pl.when(jnp.logical_not(wraps[1 - i]) | poles[k])
                def _():
                    do(corner(c, i, k))

    def each_cut(c, do):
        for i in range(2):
            for k in range(2):
                @pl.when(wraps[i] & jnp.logical_not(poles[1 - k]))
                def _():
                    do(cut(c, i, k))

    def wait_corners(c):
        for i in range(2):
            for k in range(2):
                corner(c, i, k).wait_recv()

    def start(copies):
        for copy in copies:
            copy.start()

    def arrived(copies):
        for copy in copies:
            copy.wait_recv()

    def pack(s):
        east, west = pack_matrix(2), pack_matrix(0)
        for a in (2 * s, 2 * s + 1):
            for p in range(pairs):
                block = inputs[a, :, 128 * p:128 * (p + 1)]
                ext[a, p, 0:OWN, :] = block
                snd_side[0, a, p] = dot(east, block).astype(BF16)
                snd_side[1, a, p] = dot(west, block).astype(BF16)

    def send_corners(c):
        wait_strips(c)
        east, west = corner_matrix(2), corner_matrix(0)
        for a in (2 * (c // 2), 2 * (c // 2) + 1):
            for p in range(half * (c % 2), half * (c % 2) + half):
                block = ext[a, p, NN:WW, :]
                snd_corner[0, a, p] = dot(east, block).astype(BF16)
                snd_corner[1, a, p] = dot(west, block).astype(BF16)
        each_corner(c, lambda copy: copy.start())

    def land_sides(c):
        arrived(sides(c))
        each_cut(c, lambda copy: copy.start())

    for load in loads:
        load.wait()
    pack(0)
    pack(1)
    pl.semaphore_wait(barrier, len(GREETED))
    start_detours()
    start_strips(0)
    start_strips(1)
    start(sides(0))
    row, col, ok = ext_coords(iota((8, EXT), 1))
    row, col, ok = row[0:1], col[0:1], jnp.where(ok, 1, 0)[0:1]
    token = iota((OWN, EXT), 0)
    near = (jnp.abs(col - (token & 7)) <= RADIUS) & (ok > 0)
    own_row = first + (token >> 3)
    ext_row = first + row
    begin = jnp.clip(own_row - RADIUS, 0, total_rows - 2 * RADIUS - 1)
    inside = near & (ext_row >= begin) & (ext_row <= begin + 2 * RADIUS)
    bias1[...] = jnp.where(inside, 0.0, NEG)
    begin = jnp.clip(ext_row - RADIUS, 0, total_rows - 2 * RADIUS - 1)
    inside = near & (own_row >= begin) & (own_row <= begin + 2 * RADIUS)
    inside = inside & (ext_row >= 0) & (ext_row < total_rows)
    bias2[...] = jnp.where(inside, 0.0, NEG)

    up, down = jnp.where(row < 0, -3, 0), jnp.where(row >= ROWS, 3, 0)
    left, right = jnp.where(col < 0, -1, 0), jnp.where(col >= COLS, 1, 0)
    src = (4 + up + down + left + right) * OWN + (row & (ROWS - 1)) * 8 + (col & (COLS - 1))
    src = jnp.where(ok > 0, src, -1)
    for b in range(9):
        at = iota((OWN, EXT), 0) + b * OWN
        perm[b * OWN:(b + 1) * OWN, :] = jnp.where(at == src, 1.0, 0.0).astype(BF16)

    pass_on(0)
    pass_on(1)
    start(sides(1))
    start_strips(2)
    start_strips(3)
    pass_on(2)
    pass_on(3)
    start(sides(2))
    send_corners(0)
    send_corners(1)
    start(sides(3))
    land_sides(0)
    land_sides(1)
    land_sides(2)
    send_corners(2)
    lane = iota((1, 128), 1)
    lo = jnp.where(lane < HEAD, 1.0, 0.0).astype(BF16)
    hi = jnp.where(lane < HEAD, 0.0, 1.0).astype(BF16)
    lower = iota((OWN, 128), 1) < HEAD

    def by_head(v):
        return jnp.concatenate([v * lo, v * hi], axis=0)

    def merged(v):
        return jnp.where(lower, v[:OWN], v[OWN:])

    def lanes(p):
        return pl.ds(pl.multiple_of(p * 128, 128), 128)

    def forward(p, carry):
        kx, vx = ext[0, p], ext[1, p]
        s = dot_t(by_head(ext[2, p, 0:OWN, :]), kx)
        dw = dot_t(by_head(ext[3, p, 0:OWN, :]), vx)
        at = 2 * lax.rem(p, half)
        acc = stat_acc[...]
        lane_at = iota((OWN, 128), 1)
        rounded, grads = [], []
        for h in range(2):
            of = slice(h * OWN, (h + 1) * OWN)
            t = s[of] * (scale * LOG2E) + bias1[...]
            m = jnp.max(t, axis=1, keepdims=True)
            e = jnp.exp2(t - m)
            total = jnp.sum(e, axis=1, keepdims=True)
            w = e * (1.0 / total)
            rounded.append(w.astype(BF16))
            g = dw[of]
            delta = jnp.sum(w * g, axis=1, keepdims=True)
            grads.append((w * (g - delta)).astype(BF16))
            acc = jnp.where(lane_at == at + h, m + jnp.log2(total), acc)
            acc = jnp.where(lane_at == pairs + at + h, delta, acc)
        stat_acc[...] = acc
        o = dot(jnp.concatenate(rounded, axis=0), vx)
        dq = dot(jnp.concatenate(grads, axis=0), kx)
        outputs[0, :, lanes(p)] = merged(o).astype(BF16)
        outputs[1, :, lanes(p)] = (merged(dq) * scale).astype(BF16)
        return carry

    def backward(p, carry):
        qx, cx = ext[2, p], ext[3, p]
        s = dot_t(by_head(ext[0, p, 0:OWN, :]), qx)
        dw = dot_t(by_head(ext[1, p, 0:OWN, :]), cx)
        rounded, grads = [], []
        for h in range(2):
            of = slice(h * OWN, (h + 1) * OWN)
            norm = stat_ext[2 * p + h]
            delta = stat_ext[heads + 2 * p + h]
            w = jnp.exp2(s[of] * (scale * LOG2E) + bias2[...] - norm)
            rounded.append(w.astype(BF16))
            grads.append((w * (dw[of] - delta)).astype(BF16))
        dv = dot(jnp.concatenate(rounded, axis=0), cx)
        dk = dot(jnp.concatenate(grads, axis=0), qx)
        outputs[3, :, lanes(p)] = merged(dv).astype(BF16)
        outputs[2, :, lanes(p)] = (merged(dk) * scale).astype(BF16)
        return carry

    def stats(i):
        return [remote(stat_own.at[i], stat_in.at[i, n], stat_s.at[i, n], stat_r.at[i, n], device(-a, -b))
                for n, (a, b) in enumerate(AROUND)]

    def send_stats(i):
        stat_own[i] = stat_acc[...].T[0:heads]
        start(stats(i))

    def spread_stats(i):
        arrived(stats(i))
        whole = jnp.concatenate([stat_in[i, n] for n in range(4)] + [stat_own[i]]
                                + [stat_in[i, n] for n in range(4, 8)], axis=1)
        x1 = whole.astype(BF16)
        rest = whole - x1.astype(F32)
        x2 = rest.astype(BF16)
        x3 = (rest - x2.astype(F32)).astype(BF16)
        y = dot(jnp.concatenate([x1, x2, x3], axis=0), perm[...])
        y = (y[0:heads] + y[heads:2 * heads]) + y[2 * heads:3 * heads]
        for k in range(pairs):
            stat_ext[pairs * i + k] = y[k:k + 1]
            stat_ext[heads + pairs * i + k] = y[pairs + k:pairs + k + 1]

    stat_acc[...] = jnp.zeros_like(stat_acc)
    wait_corners(0)
    lax.fori_loop(0, half, forward, 0, unroll=4)
    send_stats(0)
    land_sides(3)
    send_corners(3)
    wait_corners(1)
    lax.fori_loop(half, pairs, forward, 0, unroll=4)
    send_stats(1)
    spread_stats(0)
    wait_corners(2)
    lax.fori_loop(0, half, backward, 0, unroll=4)
    spread_stats(1)
    wait_corners(3)
    lax.fori_loop(half, pairs, backward, 0, unroll=4)

    for c in range(4):
        sent_strips(c)
        each_corner(c, lambda copy: copy.wait_send())
        each_cut(c, lambda copy: copy.wait_send())
        for copy in sides(c):
            copy.wait_send()
    for i in range(2):
        for copy in stats(i):
            copy.wait_send()


def handed_out(outputs, o_hbm, dq_hbm, dk_hbm, dv_hbm, sem):
    stores = [pltpu.make_async_copy(outputs.at[i], ref, sem.at[i])
              for i, ref in enumerate((o_hbm, dq_hbm, dk_hbm, dv_hbm))]
    for store in stores:
        store.start()
    for store in stores:
        store.wait()


def solution(mesh):
    n_lat, n_lon = mesh.shape["lat"], mesh.shape["lon"]

    def shards(queries, keys, values, cotangent):
        width = queries.shape[2]
        pairs = width // 128
        heads = 2 * pairs
        flat = [x.reshape(OWN, width) for x in (queries, keys, values, cotangent)]
        flat = [pltpu.with_memory_space_constraint(x, pltpu.HBM) for x in flat]
        dma = pltpu.SemaphoreType.DMA
        outs = pl.pallas_call(
            functools.partial(kernel, n_lat, n_lon, pairs),
            out_shape=jax.ShapeDtypeStruct((4, OWN, width), BF16),
            in_specs=[pl.BlockSpec(memory_space=pltpu.HBM)] * 4,
            out_specs=pl.BlockSpec(memory_space=pltpu.VMEM),
            scratch_shapes=[
                pltpu.VMEM((4, OWN, width), BF16),
                pltpu.VMEM((4, pairs, EXT, 128), BF16),
                pltpu.VMEM((2, 4, pairs, 96, 128), BF16),
                pltpu.VMEM((2, 4, pairs, 96, 128), BF16),
                pltpu.VMEM((4, 2, 2, 2, 48, 128), BF16),
                pltpu.VMEM((OWN, EXT), F32),
                pltpu.VMEM((OWN, EXT), F32),
                pltpu.VMEM((9 * OWN, EXT), BF16),
                pltpu.VMEM((OWN, 128), F32),
                pltpu.VMEM((2, heads, OWN), F32),
                pltpu.VMEM((2, 8, heads, OWN), F32),
                pltpu.VMEM((2 * heads, 1, EXT), F32),
                dma((4,)), dma((4, 2)), dma((4, 2)), dma((4, 2, 2)), dma((4, 2, 2)), dma((4, 2, 2)),
                dma((4, 2, XS)), dma((4, 2, XS)), dma((4, 2)), dma((4, 2)), dma((2, 8)), dma((2, 8)),
            ],
            compiler_params=pltpu.CompilerParams(
                collective_id=0, has_side_effects=True, vmem_limit_bytes=48 * 1024 * 1024),
        )(*flat)
        outs = pl.pallas_call(
            handed_out,
            out_shape=[jax.ShapeDtypeStruct((OWN, width), BF16)] * 4,
            in_specs=[pl.BlockSpec(memory_space=pltpu.VMEM)],
            out_specs=[pl.BlockSpec(memory_space=pltpu.HBM)] * 4,
            scratch_shapes=[dma((4,))],
        )(outs)
        return tuple(x.reshape(ROWS, COLS, width) for x in outs)

    spec = P("lat", "lon", None)
    return jax.shard_map(shards, mesh=mesh, in_specs=(spec,) * 4, out_specs=(spec,) * 4, check_vma=False)
```
